512 devices in a mesh: ctx: 32 (over x, z_lo), head: 4 (over z_hi, core), roll: 4 (over y).
Axes of the slice: x: 4, y: 4, z: 16 (z_hi: 2, z_lo: 8; z = z_hi * 8 + z_lo), core: 2. Of those that a mesh axis runs over, the one named last changes fastest.
Arguments:
- queries: bfloat16 [4, 8, 256, 128], P('roll', 'head', 'ctx'), may hold values from -80 to 80
- cache_keys: bfloat16 [4, 8, 98304, 128], P('roll', 'head', 'ctx'), may hold values from -4.5 to 4.5
- cache_values: bfloat16 [4, 8, 98304, 128], P('roll', 'head', 'ctx'), may hold values from -6 to 6
- new_keys: bfloat16 [4, 8, 16, 128], P('roll', 'head'), may hold values from -12 to 12
- new_values: bfloat16 [4, 8, 16, 128], P('roll', 'head'), may hold values from -6 to 6
- lengths: int32 [4], P('roll'), may hold values from 49152 to 98304, as said below
- positions: int32 [4, 16], P('roll'), may hold values from 49152 to 98319, as said below
- out_weight: bfloat16 [16384, 16384], P('head', ('ctx', 'roll')), may hold values from -0.046875 to 0.046875
Outputs:
- projected: bfloat16 [4, 16, 16384], P('head', None, ('ctx', 'roll'))
The draws below stay inside these ranges and needn't reach their ends.
Inputs may be any that keep to these rules, and one draw needn't show every extreme that they name: `lengths`: at least one rollout has the full 98304 slots. positions[r] is lengths[r] plus a permutation of 0 .. 15.
All inputs are finite; a program needn't handle non-finite values.
Results may differ from the reference program's by a relative error of at most 0.04.
Values may be sent and summed in bfloat16 or wider, within the bound.
No kernel may reach another device: no remote copies, remote signals or barrier semaphores. Data moves between devices by JAX's collectives and lax.ppermute only.
A program may use at most 64 MiB of HBM per device.

```python
import jax
import jax.numpy as jnp
from jax import lax

D = 16384
QH = 128
KVH = 8
DH = 128
NEW = 16
QPK = 16
CACHE = 98304
ROLL = 4


def shared_keys(key):
    base = jax.random.fold_in(key, 11)
    return jnp.clip(jax.random.normal(base, (ROLL, KVH, CACHE, DH), jnp.float32), -4.5, 4.5)


def rollout_bounds(key):
    lengths = jax.random.randint(jax.random.fold_in(key, 21), (ROLL,), CACHE // 2, CACHE + 1)
    filled = jax.random.randint(jax.random.fold_in(key, 22), (), 0, ROLL)
    lengths = jnp.where(jnp.arange(ROLL) == filled, CACHE, lengths).astype(jnp.int32)
    orders = jax.vmap(lambda sub: jax.random.permutation(sub, NEW))(jax.random.split(jax.random.fold_in(key, 23), ROLL))
    positions = lengths[:, None] + orders.astype(jnp.int32)
    return (lengths, positions.astype(jnp.int32))


def draw_cache_keys(key, part):
    keys = shared_keys(key)
    return keys.astype(jnp.bfloat16)


def draw_queries(key, part):
    key = jax.random.fold_in(key, 2)
    rows = NEW * QPK
    values = 3.0 * jnp.clip(jax.random.normal(key, (ROLL, KVH, rows, DH), jnp.float32), -4.0, 4.0)
    return values.astype(jnp.bfloat16)


def draw_lengths(key, part):
    lengths, positions = rollout_bounds(key)
    return lengths


def draw_positions(key, part):
    lengths, positions = rollout_bounds(key)
    return positions


def block_scale(key, extent, shards, smallest, largest):
    def one(axis_at, blocks):
        steps = jax.random.uniform(jax.random.fold_in(jax.random.fold_in(key, 6), axis_at), (blocks,), jnp.float32, smallest / len(shards), largest / len(shards))
        return jnp.repeat(jnp.exp(steps), extent[axis_at] // blocks).reshape((-1,) + (1,) * (len(extent) - axis_at - 1))

    level = one(*shards[0])
    for cut in shards[1:]:
        level = level * one(*cut)
    return level


def normal_values(rng, extent, width, limit, pieces=(), kind=jnp.bfloat16):
    array = jax.random.normal(rng, extent, jnp.float32) * width
    if len(pieces) > 0:
        array = block_scale(rng, extent, pieces, -0.22, 0.18) * array
    return jnp.clip(array, min=-limit, max=limit).astype(kind)


def setup_inputs(seed: int = 0) -> dict:
    key_of = jax.random.split(jax.random.key(seed), 9)
    return {
        "queries": draw_queries(jax.random.fold_in(key_of[8], 71), 0),
        "cache_keys": draw_cache_keys(jax.random.fold_in(key_of[8], 71), 0),
        "cache_values": normal_values(key_of[2], (ROLL, KVH, CACHE, DH), 1.0, 6.0, ((0, 4), (1, 4), (2, 32))),
        "new_keys": normal_values(key_of[3], (ROLL, KVH, NEW, DH), 2.5, 12.0, ((0, 4), (1, 4))),
        "new_values": normal_values(key_of[4], (ROLL, KVH, NEW, DH), 1.0, 6.0, ((0, 4), (1, 4))),
        "lengths": draw_lengths(jax.random.fold_in(key_of[8], 71), 0),
        "positions": draw_positions(jax.random.fold_in(key_of[8], 71), 0),
        "out_weight": normal_values(key_of[7], (QH * DH, D), (QH * DH) ** -0.5, 0.046875, ((0, 4), (1, 128))),
    }


NEG = -1.0e30


def attend_one(items):
    query, keys, values, fresh_keys, fresh_values, length, pos = items
    scale = 1.0 / (DH ** 0.5)
    scores = jnp.dot(query, keys.T, preferred_element_type=jnp.float32) * scale
    keep = jnp.arange(CACHE) < length
    scores = jnp.where(keep[None, :], scores, NEG)
    fresh = jnp.dot(query, fresh_keys.T, preferred_element_type=jnp.float32) * scale
    token = jnp.arange(NEW * QPK) // QPK
    allow = pos[None, :] <= pos[token][:, None]
    fresh = jnp.where(allow, fresh, NEG)
    top = jnp.maximum(jnp.max(scores, axis=1), jnp.max(fresh, axis=1))
    cache_weights = jnp.where(keep[None, :], jnp.exp(scores - top[:, None]), 0.0).astype(jnp.bfloat16)
    fresh_weights = jnp.where(allow, jnp.exp(fresh - top[:, None]), 0.0).astype(jnp.bfloat16)
    total = jnp.sum(cache_weights.astype(jnp.float32), axis=1) + jnp.sum(fresh_weights.astype(jnp.float32), axis=1)
    summed = jnp.dot(cache_weights, values, preferred_element_type=jnp.float32)
    summed = summed + jnp.dot(fresh_weights, fresh_values, preferred_element_type=jnp.float32)
    return (summed / total[:, None]).astype(jnp.bfloat16)


def reference(queries, cache_keys, cache_values, new_keys, new_values, lengths, positions, out_weight):
    flat = ROLL * KVH
    items = (
        queries.reshape(flat, NEW * QPK, DH),
        cache_keys.reshape(flat, CACHE, DH),
        cache_values.reshape(flat, CACHE, DH),
        new_keys.reshape(flat, NEW, DH),
        new_values.reshape(flat, NEW, DH),
        jnp.repeat(lengths, KVH),
        jnp.repeat(positions, KVH, axis=0),
    )
    attended = lax.map(attend_one, items)
    attended = attended.reshape(ROLL, KVH, NEW, QPK, DH).transpose(0, 2, 1, 3, 4)
    features = attended.reshape(ROLL * NEW, QH * DH)
    projected = jnp.dot(features, out_weight, preferred_element_type=jnp.float32)
    return projected.astype(jnp.bfloat16).reshape(ROLL, NEW, D)
```

```python
import functools
import math

import jax
import jax.numpy as jnp
from jax import lax
from jax.experimental import pallas as pl
from jax.experimental.pallas import tpu as pltpu
from jax.sharding import Mesh
from jax.sharding import PartitionSpec as P

NEW = 16
QPK = 16
NEG = -1e30
CTX = ("x", "zl")
HEAD = ("zh", "core")
BF = jnp.bfloat16
F32 = jnp.float32
STAT_ROWS = 16


def iota(shape, dim):
    return lax.broadcasted_iota(jnp.int32, shape, dim)


def dot_nt(a, b):
    return lax.dot_general(a, b, (((1,), (1,)), ((), ())), preferred_element_type=F32)


def split3(row):
    hi = row.astype(BF).astype(F32)
    rest = row - hi
    mid = rest.astype(BF).astype(F32)
    return hi, mid, rest - mid


def pack_stats(top, total):
    rows = split3(top) + split3(total)
    at = iota((STAT_ROWS, top.shape[1]), 0)
    out = jnp.zeros((STAT_ROWS, top.shape[1]), F32)
    for n, row in enumerate(rows):
        out = jnp.where(at == n, row, out)
    return out.astype(BF)


def unpack_stats(tile):
    rows = tile.astype(F32)
    top = (rows[0:1] + rows[1:2]) + rows[2:3]
    total = (rows[3:4] + rows[4:5]) + rows[5:6]
    return top, total


def attend_kernel(info, q_ref, keys, values, fresh_keys, fresh_values, pos_ref, out_ref, scores, *, rate, chunk):
    heads, slots, size = keys.shape
    n_rows = heads * NEW * QPK
    rows = NEW * QPK
    valid = info[0]
    fresh_on = info[1]
    queries = q_ref[...].reshape(n_rows, size)
    dest = iota((n_rows, 1), 0)
    head, j, token = dest // rows, (dest // NEW) % QPK, dest % NEW
    half_rows = QPK // 2
    source = (token * 2 + j // half_rows) * (heads * half_rows) + head * half_rows + j % half_rows
    order = jnp.where(iota((n_rows, n_rows), 1) == source, 1.0, 0.0).astype(BF)
    queries = jnp.dot(order, queries, preferred_element_type=F32).astype(BF)

    pos = jnp.broadcast_to(pos_ref[...], (rows, NEW))
    mine = jnp.where(iota((rows, NEW), 0) % NEW == iota((rows, NEW), 1), pos, 0)
    allow = jnp.logical_and(pos <= jnp.sum(mine, axis=1, keepdims=True), fresh_on > 0)

    for k in range(heads):
        q = queries[k * rows : (k + 1) * rows]
        fresh = jnp.where(allow, dot_nt(q, fresh_keys[k]), NEG)
        part = jnp.full((rows, 128), NEG, F32)
        for c in range(slots // chunk):
            s = dot_nt(q, keys[k, pl.ds(c * chunk, chunk), :])
            s = jnp.where(iota((1, chunk), 1) + c * chunk < valid, s, NEG)
            scores[:, pl.ds(c * chunk, chunk)] = s
            for i in range(chunk // 128):
                part = jnp.maximum(part, s[:, i * 128 : (i + 1) * 128])
        top = jnp.maximum(jnp.max(part, axis=1, keepdims=True), jnp.max(fresh, axis=1, keepdims=True))
        weights = jnp.exp2((fresh - top) * rate).astype(BF)
        fresh_ones = jnp.concatenate([fresh_values[k], jnp.ones((NEW, size), BF)], axis=1)
        acc = jnp.dot(weights, fresh_ones, preferred_element_type=F32)
        for c in range(slots // chunk):
            w = jnp.exp2((scores[:, pl.ds(c * chunk, chunk)] - top) * rate).astype(BF)
            v = jnp.concatenate([values[k, pl.ds(c * chunk, chunk), :], jnp.ones((chunk, size), BF)], axis=1)
            acc = acc + jnp.dot(w, v, preferred_element_type=F32)
        total = acc[:, size:]
        attended = (acc[:, :size] / total).astype(BF)
        for h in range(2):
            part_rows = slice(h * 128, (h + 1) * 128)
            lane = iota((128, 128), 1)
            cols = jnp.where(lane == 0, top[part_rows], total[part_rows])
            stats = jnp.transpose(cols)
            out_ref[2 * k + h, 0:128, :] = attended[part_rows]
            out_ref[2 * k + h, 128:, :] = pack_stats(stats[0:1], stats[1:2])


def combine_kernel(r_ref, out_ref, *, rate, last):
    sources = r_ref.shape[0]
    copies = out_ref.shape[0]
    stats = [unpack_stats(r_ref[s, 128:, :]) for s in range(sources)]
    top = functools.reduce(jnp.maximum, [m for m, _ in stats])
    weights = [t * jnp.exp2((m - top) * rate) for m, t in stats]
    total = functools.reduce(jnp.add, weights)
    at = iota((128, 128), 0)
    factors = jnp.zeros((128, 128), F32)
    for s in range(sources):
        factors = jnp.where(at == s, weights[s] / total, factors)
    factors = jnp.transpose(factors)
    out = jnp.zeros((128, 128), F32)
    for s in range(sources):
        out = out + factors[:, s : s + 1] * r_ref[s, 0:128, :].astype(F32)
    out = out.astype(BF)
    for c in range(copies):
        out_ref[c, 0:128, :] = out
    if not last:
        tail = pack_stats(top, total)
        for c in range(copies):
            out_ref[c, 128:, :] = tail


def project_kernel(r_ref, w_ref, out_ref):
    n_x, n_y, rows, size = r_ref.shape
    per = rows // NEW
    acc = jnp.zeros((n_y * NEW, w_ref.shape[1]), F32)
    for x in range(n_x):
        for j in range(0, per, 2):
            block = jnp.concatenate(
                [
                    jnp.concatenate([r_ref[x, y, pl.ds((j + i) * NEW, NEW), :] for y in range(n_y)], axis=0)
                    for i in range(2)
                ],
                axis=1,
            )
            acc = acc + jnp.dot(
                block, w_ref[pl.ds((x * per + j) * size, 2 * size), :], preferred_element_type=F32
            )
    out_ref[...] = acc.astype(BF).reshape(out_ref.shape)


def in_vmem(n):
    return [pl.BlockSpec(memory_space=pltpu.VMEM)] * n


def attend(info, q, keys, values, fresh_keys, fresh_values, pos):
    heads, slots, size = keys.shape
    rate = math.log2(math.e) / size**0.5
    chunk = min(slots, 512)
    flops = 4 * heads * NEW * QPK * slots * size
    return pl.pallas_call(
        functools.partial(attend_kernel, rate=rate, chunk=chunk),
        out_shape=jax.ShapeDtypeStruct((2 * heads, 128 + STAT_ROWS, size), BF),
        in_specs=[pl.BlockSpec(memory_space=pltpu.SMEM)] + in_vmem(6),
        out_specs=pl.BlockSpec(memory_space=pltpu.VMEM),
        scratch_shapes=[pltpu.VMEM((NEW * QPK, slots), F32)],
        compiler_params=pltpu.CompilerParams(vmem_limit_bytes=24 << 20),
        cost_estimate=pl.CostEstimate(
            flops=flops, bytes_accessed=2 * heads * slots * size * 2, transcendentals=heads * NEW * QPK * slots
        ),
        name="attend",
    )(info, q, keys, values, fresh_keys, fresh_values, pos)


def combine(r, copies, last, rate):
    rows = 128 if last else 128 + STAT_ROWS
    return pl.pallas_call(
        functools.partial(combine_kernel, rate=rate, last=last),
        out_shape=jax.ShapeDtypeStruct((copies, rows, r.shape[2]), BF),
        in_specs=in_vmem(1),
        out_specs=pl.BlockSpec(memory_space=pltpu.VMEM),
        name="combine_last" if last else "combine",
    )(r)


def project(r, w):
    return pl.pallas_call(
        project_kernel,
        out_shape=jax.ShapeDtypeStruct((r.shape[1], NEW, w.shape[1]), BF),
        in_specs=in_vmem(2),
        out_specs=pl.BlockSpec(memory_space=pltpu.VMEM),
        name="project",
    )(r, w)


def body(queries, cache_keys, cache_values, new_keys, new_values, lengths, positions, out_weight):
    size = cache_keys.shape[3]
    slots = cache_keys.shape[2]
    rate = math.log2(math.e) / size**0.5
    n_ctx = lax.axis_size(CTX)
    here = lax.axis_index(CTX)
    info = jnp.stack([lengths[0] - here * slots, (here == 0).astype(jnp.int32)])
    mine = queries[0].reshape(1, -1, size)
    sent = jnp.broadcast_to(mine, (n_ctx,) + mine.shape[1:])
    q = lax.all_to_all(sent, CTX, 0, 0, tiled=True)
    part = attend(info, q, cache_keys[0], cache_values[0], new_keys[0], new_values[0], positions)
    part = lax.all_to_all(part, "x", 0, 0, tiled=True)
    part = combine(part, lax.axis_size("zl"), False, rate)
    part = lax.all_to_all(part, "zl", 0, 0, tiled=True)
    n_x, n_y = lax.axis_size("x"), lax.axis_size("y")
    rows = combine(part, n_x * n_y, True, rate)
    rows = lax.all_to_all(rows, ("x", "y"), 0, 0, tiled=True)
    out = project(rows.reshape(n_x, n_y, *rows.shape[1:]), out_weight)
    every = lax.all_gather(out, HEAD, axis=0)
    mine = lax.dynamic_index_in_dim(every, lax.axis_index(HEAD), 1, keepdims=True)
    return jnp.sum(mine.astype(F32), axis=0).astype(BF)


def solution(mesh):
    fine = Mesh(mesh.devices.reshape(4, 8, 2, 2, 4), ("x", "zl", "zh", "core", "y"))
    in_specs = (
        P("y", HEAD, CTX, None),
        P("y", HEAD, CTX, None),
        P("y", HEAD, CTX, None),
        P("y", HEAD, None, None),
        P("y", HEAD, None, None),
        P("y"),
        P("y", None),
        P(HEAD, CTX + ("y",)),
    )
    out_specs = P(HEAD, None, CTX + ("y",))
    return jax.shard_map(body, mesh=fine, in_specs=in_specs, out_specs=out_specs, check_vma=False)
```

```python
import functools
import math

import jax
import jax.numpy as jnp
from jax import lax
from jax.experimental import pallas as pl
from jax.experimental.pallas import tpu as pltpu
from jax.sharding import Mesh
from jax.sharding import PartitionSpec as P

NEW = 16
QPK = 16
NEG = -1e30
Z = ("za", "zb")
CTX = ("x",) + Z
HEAD = ("zh", "core")
BF = jnp.bfloat16
F32 = jnp.float32
STAT_ROWS = 16


def iota(shape, dim):
    return lax.broadcasted_iota(jnp.int32, shape, dim)


def dot_nt(a, b):
    return lax.dot_general(a, b, (((1,), (1,)), ((), ())), preferred_element_type=F32)


def split3(row):
    hi = row.astype(BF).astype(F32)
    rest = row - hi
    mid = rest.astype(BF).astype(F32)
    return hi, mid, rest - mid


def pack_stats(top, total):
    rows = split3(top) + split3(total)
    at = iota((STAT_ROWS, top.shape[1]), 0)
    out = jnp.zeros((STAT_ROWS, top.shape[1]), F32)
    for n, row in enumerate(rows):
        out = jnp.where(at == n, row, out)
    return out.astype(BF)


def unpack_stats(tile):
    rows = tile.astype(F32)
    top = (rows[0:1] + rows[1:2]) + rows[2:3]
    total = (rows[3:4] + rows[4:5]) + rows[5:6]
    return top, total


def attend_kernel(info, q_ref, keys, values, fresh_keys, fresh_values, pos_ref, out_ref, scores, *, rate, chunk):
    heads, slots, size = keys.shape
    n_rows = heads * NEW * QPK
    rows = NEW * QPK
    valid = info[0]
    fresh_on = info[1]
    queries = q_ref[...].reshape(n_rows, size)
    dest = iota((n_rows, 1), 0)
    head, j, token = dest // rows, (dest // NEW) % QPK, dest % NEW
    half_rows = QPK // 2
    source = (token * 2 + j // half_rows) * (heads * half_rows) + head * half_rows + j % half_rows
    order = jnp.where(iota((n_rows, n_rows), 1) == source, 1.0, 0.0).astype(BF)
    queries = jnp.dot(order, queries, preferred_element_type=F32).astype(BF)

    pos = jnp.broadcast_to(pos_ref[...], (rows, NEW))
    mine = jnp.where(iota((rows, NEW), 0) % NEW == iota((rows, NEW), 1), pos, 0)
    allow = jnp.logical_and(pos <= jnp.sum(mine, axis=1, keepdims=True), fresh_on > 0)

    for k in range(heads):
        q = queries[k * rows : (k + 1) * rows]
        fresh = jnp.where(allow, dot_nt(q, fresh_keys[k]), NEG)
        part = jnp.full((rows, 128), NEG, F32)
        for c in range(slots // chunk):
            s = dot_nt(q, keys[k, pl.ds(c * chunk, chunk), :])
            s = jnp.where(iota((1, chunk), 1) + c * chunk < valid, s, NEG)
            scores[:, pl.ds(c * chunk, chunk)] = s
            for i in range(chunk // 128):
                part = jnp.maximum(part, s[:, i * 128 : (i + 1) * 128])
        top = jnp.maximum(jnp.max(part, axis=1, keepdims=True), jnp.max(fresh, axis=1, keepdims=True))
        weights = jnp.exp2((fresh - top) * rate).astype(BF)
        fresh_ones = jnp.concatenate([fresh_values[k], jnp.ones((NEW, size), BF)], axis=1)
        acc = jnp.dot(weights, fresh_ones, preferred_element_type=F32)
        for c in range(slots // chunk):
            w = jnp.exp2((scores[:, pl.ds(c * chunk, chunk)] - top) * rate).astype(BF)
            v = jnp.concatenate([values[k, pl.ds(c * chunk, chunk), :], jnp.ones((chunk, size), BF)], axis=1)
            acc = acc + jnp.dot(w, v, preferred_element_type=F32)
        total = acc[:, size:]
        attended = (acc[:, :size] / total).astype(BF)
        for h in range(2):
            part_rows = slice(h * 128, (h + 1) * 128)
            lane = iota((128, 128), 1)
            cols = jnp.where(lane == 0, top[part_rows], total[part_rows])
            stats = jnp.transpose(cols)
            out_ref[2 * k + h, 0:128, :] = attended[part_rows]
            out_ref[2 * k + h, 128:, :] = pack_stats(stats[0:1], stats[1:2])


def combine_kernel(r_ref, out_ref, *, rate, last):
    sources = r_ref.shape[0]
    copies = out_ref.shape[0]
    rows = r_ref.shape[1] - STAT_ROWS
    size = r_ref.shape[2]
    stats = [unpack_stats(r_ref[s, rows:, :]) for s in range(sources)]
    top = functools.reduce(jnp.maximum, [m for m, _ in stats])
    weights = [t * jnp.exp2((m - top) * rate) for m, t in stats]
    total = functools.reduce(jnp.add, weights)
    at = iota((size, size), 0)
    factors = jnp.zeros((size, size), F32)
    for s in range(sources):
        factors = jnp.where(at == s, weights[s] / total, factors)
    factors = jnp.transpose(factors)
    out = jnp.zeros((rows, size), F32)
    for s in range(sources):
        out = out + factors[0:rows, s : s + 1] * r_ref[s, 0:rows, :].astype(F32)
    out = out.astype(BF)
    if last:
        for c in range(copies):
            out_ref[c] = out
        return
    half = rows // 2
    for h in range(2):
        if h:
            top, total = (jnp.concatenate([v[:, half:], v[:, :half]], axis=1) for v in (top, total))
        tail = pack_stats(top, total)
        for c in range(h, copies, 2):
            out_ref[c, 0:half, :] = out[h * half : (h + 1) * half]
            out_ref[c, half:, :] = tail


def project_kernel(r_ref, w_ref, out_ref):
    n_x, n_y, n_z, rows, size = r_ref.shape
    per = rows // NEW
    acc = jnp.zeros((n_y * NEW, w_ref.shape[1]), F32)
    for x in range(n_x):
        for z in range(n_z):
            for j in range(0, per, 2):
                block = jnp.concatenate(
                    [
                        jnp.concatenate([r_ref[x, y, z, pl.ds((j + i) * NEW, NEW), :] for y in range(n_y)], axis=0)
                        for i in range(2)
                    ],
                    axis=1,
                )
                start = ((x * n_z + z) * per + j) * size
                acc = acc + jnp.dot(block, w_ref[pl.ds(start, 2 * size), :], preferred_element_type=F32)
    out_ref[...] = acc.astype(BF).reshape(out_ref.shape)


def in_vmem(n):
    return [pl.BlockSpec(memory_space=pltpu.VMEM)] * n


def stage_kernel(*refs):
    count = (len(refs) - 1) // 2
    copies = [pltpu.make_async_copy(refs[n], refs[count + n], refs[-1].at[n]) for n in range(count)]
    for copy in copies:
        copy.start()
    for copy in copies:
        copy.wait()


def stage(*arrays):
    return pl.pallas_call(
        stage_kernel,
        out_shape=[jax.ShapeDtypeStruct(a.shape, a.dtype) for a in arrays],
        in_specs=[pl.BlockSpec(memory_space=pltpu.HBM)] * len(arrays),
        out_specs=in_vmem(len(arrays)),
        scratch_shapes=[pltpu.SemaphoreType.DMA((len(arrays),))],
        compiler_params=pltpu.CompilerParams(vmem_limit_bytes=8 << 20),
        cost_estimate=pl.CostEstimate(flops=0, bytes_accessed=2 * sum(a.size * 2 for a in arrays), transcendentals=0),
        name="stage",
    )(*[pltpu.with_memory_space_constraint(a, pltpu.HBM) for a in arrays])


def attend(info, q, keys, values, fresh_keys, fresh_values, pos):
    heads, slots, size = keys.shape
    rate = math.log2(math.e) / size**0.5
    chunk = min(slots, 512)
    flops = 4 * heads * NEW * QPK * slots * size
    return pl.pallas_call(
        functools.partial(attend_kernel, rate=rate, chunk=chunk),
        out_shape=jax.ShapeDtypeStruct((2 * heads, 128 + STAT_ROWS, size), BF),
        in_specs=[pl.BlockSpec(memory_space=pltpu.SMEM)] + in_vmem(6),
        out_specs=pl.BlockSpec(memory_space=pltpu.VMEM),
        scratch_shapes=[pltpu.VMEM((NEW * QPK, slots), F32)],
        compiler_params=pltpu.CompilerParams(vmem_limit_bytes=16 << 20),
        cost_estimate=pl.CostEstimate(
            flops=flops, bytes_accessed=2 * heads * slots * size * 2, transcendentals=heads * NEW * QPK * slots
        ),
        name="attend",
    )(info, q, keys, values, fresh_keys, fresh_values, pos)


def combine(r, copies, last, rate):
    rows = r.shape[1] - STAT_ROWS if last else (r.shape[1] - STAT_ROWS) // 2 + STAT_ROWS
    return pl.pallas_call(
        functools.partial(combine_kernel, rate=rate, last=last),
        out_shape=jax.ShapeDtypeStruct((copies, rows, r.shape[2]), BF),
        in_specs=in_vmem(1),
        out_specs=pl.BlockSpec(memory_space=pltpu.VMEM),
        compiler_params=pltpu.CompilerParams(vmem_limit_bytes=8 << 20),
        name="combine_last" if last else "combine",
    )(r)


def project(r, w):
    return pl.pallas_call(
        project_kernel,
        out_shape=jax.ShapeDtypeStruct((r.shape[1], NEW, w.shape[1]), BF),
        in_specs=in_vmem(2),
        out_specs=pl.BlockSpec(memory_space=pltpu.VMEM),
        compiler_params=pltpu.CompilerParams(vmem_limit_bytes=8 << 20),
        name="project",
    )(r, w)


def body(queries, cache_keys, cache_values, new_keys, new_values, lengths, positions, out_weight):
    size = cache_keys.shape[3]
    slots = cache_keys.shape[2]
    rate = math.log2(math.e) / size**0.5
    n_ctx = lax.axis_size(CTX)
    here = lax.axis_index(CTX)
    info = jnp.stack([lengths[0] - here * slots, (here == 0).astype(jnp.int32)])
    mine = queries[0].reshape(1, -1, size)
    sent = jnp.broadcast_to(mine, (n_ctx,) + mine.shape[1:])
    q = lax.all_to_all(sent, CTX, 0, 0, tiled=True)
    keys, values, fresh_keys, fresh_values, pos = stage(
        cache_keys[0], cache_values[0], new_keys[0], new_values[0], positions
    )
    part = attend(info, q, keys, values, fresh_keys, fresh_values, pos)
    part = lax.all_to_all(part, "x", 0, 0, tiled=True)
    part = combine(part, lax.axis_size(Z), False, rate)
    part = lax.all_to_all(part, Z, 0, 0, tiled=True)
    spread = ("x", "y", "zb")
    sizes = tuple(lax.axis_size(a) for a in spread)
    rows = combine(part, math.prod(sizes), True, rate)
    rows = lax.all_to_all(rows, spread, 0, 0, tiled=True)
    out = project(rows.reshape(*sizes, *rows.shape[1:]), out_weight)
    every = lax.all_gather(out, HEAD, axis=0)
    mine = lax.dynamic_index_in_dim(every, lax.axis_index(HEAD), 1, keepdims=True)
    return jnp.sum(mine.astype(F32), axis=0).astype(BF)


def solution(mesh):
    fine = Mesh(mesh.devices.reshape(4, 4, 2, 2, 2, 4), ("x", "za", "zb", "zh", "core", "y"))
    in_specs = (
        P("y", HEAD, CTX, None),
        P("y", HEAD, CTX, None),
        P("y", HEAD, CTX, None),
        P("y", HEAD, None, None),
        P("y", HEAD, None, None),
        P("y"),
        P("y", None),
        P(HEAD, CTX + ("y",)),
    )
    out_specs = P(HEAD, None, CTX + ("y",))
    return jax.shard_map(body, mesh=fine, in_specs=in_specs, out_specs=out_specs, check_vma=False)
```

```python
import functools
import math

import jax
import jax.numpy as jnp
from jax import lax
from jax.experimental import pallas as pl
from jax.experimental.pallas import tpu as pltpu
from jax.sharding import Mesh
from jax.sharding import PartitionSpec as P

NEW = 16
QPK = 16
NEG = -1e30
Z = ("za", "zb")
CTX = ("x",) + Z
HEAD = ("zh", "core")
BF = jnp.bfloat16
F32 = jnp.float32
STAT_ROWS = 16


def iota(shape, dim):
    return lax.broadcasted_iota(jnp.int32, shape, dim)


def dot_nt(a, b):
    return lax.dot_general(a, b, (((1,), (1,)), ((), ())), preferred_element_type=F32)


def split3(row):
    hi = row.astype(BF).astype(F32)
    rest = row - hi
    mid = rest.astype(BF).astype(F32)
    return hi, mid, rest - mid


def pack_stats(top, total):
    rows = split3(top) + split3(total)
    at = iota((STAT_ROWS, top.shape[1]), 0)
    out = jnp.zeros((STAT_ROWS, top.shape[1]), F32)
    for n, row in enumerate(rows):
        out = jnp.where(at == n, row, out)
    return out.astype(BF)


def unpack_stats(tile):
    rows = tile.astype(F32)
    top = (rows[0:1] + rows[1:2]) + rows[2:3]
    total = (rows[3:4] + rows[4:5]) + rows[5:6]
    return top, total


def attend_kernel(info, q_ref, keys, values, fresh_keys, fresh_values, pos_ref, out_ref, scores, *, rate, chunk):
    heads, slots, size = keys.shape
    rows = NEW * QPK
    valid = info[0]
    fresh_on = info[1]
    half_rows = QPK // 2
    n = NEW * half_rows
    dest = iota((n, 1), 0)
    order = jnp.where(iota((n, n), 1) == dest % NEW * half_rows + dest // NEW, 1.0, 0.0).astype(BF)
    arrived = q_ref[...].astype(F32).reshape(NEW, 2, heads * half_rows, size)

    def ordered(k, h):
        block = arrived[:, h, k * half_rows : (k + 1) * half_rows, :].reshape(n, size).astype(BF)
        return jnp.dot(order, block, preferred_element_type=F32).astype(BF)


    pos = jnp.broadcast_to(pos_ref[...], (rows, NEW))
    mine = jnp.where(iota((rows, NEW), 0) % NEW == iota((rows, NEW), 1), pos, 0)
    allow = jnp.logical_and(pos <= jnp.sum(mine, axis=1, keepdims=True), fresh_on > 0)

    def finish(k, acc, top):
        total = acc[:, size:]
        attended = (acc[:, :size] / total).astype(BF)
        for h in range(2):
            part_rows = slice(h * 128, (h + 1) * 128)
            lane = iota((128, 128), 1)
            cols = jnp.where(lane == 0, top[part_rows], total[part_rows])
            stats = jnp.transpose(cols)
            out_ref[2 * k + h, 0:128, :] = attended[part_rows]
            out_ref[2 * k + h, 128:, :] = pack_stats(stats[0:1], stats[1:2])

    tops = []
    for k in range(heads):
        q = jnp.concatenate([ordered(k, 0), ordered(k, 1)], axis=0)
        fresh = jnp.where(allow, dot_nt(q, fresh_keys[k]), NEG)
        part = jnp.full((rows, 128), NEG, F32)
        for c in range(slots // chunk):
            s = dot_nt(q, keys[k, pl.ds(c * chunk, chunk), :])
            s = jnp.where(iota((1, chunk), 1) + c * chunk < valid, s, NEG)
            scores[k, :, pl.ds(c * chunk, chunk)] = s
            for i in range(chunk // 128):
                part = jnp.maximum(part, s[:, i * 128 : (i + 1) * 128])
        top = jnp.maximum(jnp.max(part, axis=1, keepdims=True), jnp.max(fresh, axis=1, keepdims=True))
        tops.append((top, fresh))
    for k in range(heads):
        top, fresh = tops[k]
        weights = jnp.exp2((fresh - top) * rate).astype(BF)
        fresh_ones = jnp.concatenate([fresh_values[k], jnp.ones((NEW, size), BF)], axis=1)
        acc = jnp.dot(weights, fresh_ones, preferred_element_type=F32)
        for c in range(slots // chunk):
            w = jnp.exp2((scores[k, :, pl.ds(c * chunk, chunk)] - top) * rate).astype(BF)
            v = jnp.concatenate([values[k, pl.ds(c * chunk, chunk), :], jnp.ones((chunk, size), BF)], axis=1)
            acc = acc + jnp.dot(w, v, preferred_element_type=F32)
        finish(k, acc, top)


def combine_kernel(r_ref, out_ref, *, rate, last):
    sources = r_ref.shape[0]
    copies = out_ref.shape[0]
    rows = r_ref.shape[1] - STAT_ROWS
    size = r_ref.shape[2]
    stats = [unpack_stats(r_ref[s, rows:, :]) for s in range(sources)]
    top = functools.reduce(jnp.maximum, [m for m, _ in stats])
    weights = [t * jnp.exp2((m - top) * rate) for m, t in stats]
    total = functools.reduce(jnp.add, weights)
    at = iota((size, size), 0)
    factors = jnp.zeros((size, size), F32)
    for s in range(sources):
        factors = jnp.where(at == s, weights[s] / total, factors)
    factors = jnp.transpose(factors)
    out = jnp.zeros((rows, size), F32)
    for s in range(sources):
        out = out + factors[0:rows, s : s + 1] * r_ref[s, 0:rows, :].astype(F32)
    out = out.astype(BF)
    if last:
        for c in range(copies):
            out_ref[c] = out
        return
    half = rows // 2
    for h in range(2):
        if h:
            top, total = (jnp.concatenate([v[:, half:], v[:, :half]], axis=1) for v in (top, total))
        tail = pack_stats(top, total)
        for c in range(h, copies, 2):
            out_ref[c, 0:half, :] = out[h * half : (h + 1) * half]
            out_ref[c, half:, :] = tail


def project_kernel(r_ref, w_ref, out_ref):
    n_x, n_y, n_z, rows, size = r_ref.shape
    per = rows // NEW
    acc = jnp.zeros((n_y * NEW, w_ref.shape[1]), F32)
    for x in range(n_x):
        for z in range(n_z):
            for j in range(0, per, 2):
                block = jnp.concatenate(
                    [
                        jnp.concatenate([r_ref[x, y, z, pl.ds((j + i) * NEW, NEW), :] for y in range(n_y)], axis=0)
                        for i in range(2)
                    ],
                    axis=1,
                )
                start = ((x * n_z + z) * per + j) * size
                acc = acc + jnp.dot(block, w_ref[pl.ds(start, 2 * size), :], preferred_element_type=F32)
    out_ref[...] = acc.astype(BF).reshape(out_ref.shape)


def in_vmem(n):
    return [pl.BlockSpec(memory_space=pltpu.VMEM)] * n


def stage_kernel(*refs):
    count = (len(refs) - 1) // 2
    copies = [pltpu.make_async_copy(refs[n], refs[count + n], refs[-1].at[n]) for n in range(count)]
    for copy in copies:
        copy.start()
    for copy in copies:
        copy.wait()


def stage(*arrays):
    return pl.pallas_call(
        stage_kernel,
        out_shape=[jax.ShapeDtypeStruct(a.shape, a.dtype) for a in arrays],
        in_specs=[pl.BlockSpec(memory_space=pltpu.HBM)] * len(arrays),
        out_specs=in_vmem(len(arrays)),
        scratch_shapes=[pltpu.SemaphoreType.DMA((len(arrays),))],
        compiler_params=pltpu.CompilerParams(vmem_limit_bytes=8 << 20),
        cost_estimate=pl.CostEstimate(flops=0, bytes_accessed=2 * sum(a.size * 2 for a in arrays), transcendentals=0),
        name="stage",
    )(*[pltpu.with_memory_space_constraint(a, pltpu.HBM) for a in arrays])


def attend(info, q, keys, values, fresh_keys, fresh_values, pos):
    heads, slots, size = keys.shape
    rate = math.log2(math.e) / size**0.5
    chunk = min(slots, 256)
    flops = 4 * heads * NEW * QPK * slots * size
    return pl.pallas_call(
        functools.partial(attend_kernel, rate=rate, chunk=chunk),
        out_shape=jax.ShapeDtypeStruct((2 * heads, 128 + STAT_ROWS, size), BF),
        in_specs=[pl.BlockSpec(memory_space=pltpu.SMEM)] + in_vmem(6),
        out_specs=pl.BlockSpec(memory_space=pltpu.VMEM),
        scratch_shapes=[pltpu.VMEM((heads, NEW * QPK, slots), F32)],
        compiler_params=pltpu.CompilerParams(vmem_limit_bytes=13 << 20),
        cost_estimate=pl.CostEstimate(
            flops=flops, bytes_accessed=2 * heads * slots * size * 2, transcendentals=heads * NEW * QPK * slots
        ),
        name="attend",
    )(info, q, keys, values, fresh_keys, fresh_values, pos)


def combine(r, copies, last, rate):
    rows = r.shape[1] - STAT_ROWS if last else (r.shape[1] - STAT_ROWS) // 2 + STAT_ROWS
    return pl.pallas_call(
        functools.partial(combine_kernel, rate=rate, last=last),
        out_shape=jax.ShapeDtypeStruct((copies, rows, r.shape[2]), BF),
        in_specs=in_vmem(1),
        out_specs=pl.BlockSpec(memory_space=pltpu.VMEM),
        compiler_params=pltpu.CompilerParams(vmem_limit_bytes=8 << 20),
        name="combine_last" if last else "combine",
    )(r)


def project(r, w):
    return pl.pallas_call(
        project_kernel,
        out_shape=jax.ShapeDtypeStruct((r.shape[1], NEW, w.shape[1]), BF),
        in_specs=in_vmem(2),
        out_specs=pl.BlockSpec(memory_space=pltpu.VMEM),
        compiler_params=pltpu.CompilerParams(vmem_limit_bytes=8 << 20),
        name="project",
    )(r, w)


def total_kernel(every, out_ref):
    mine = lax.axis_index(HEAD)
    total = every[0, mine].astype(F32)
    for h in range(1, every.shape[0]):
        total = total + every[h, mine].astype(F32)
    out_ref[0] = total.astype(BF)


def total_of(every):
    return pl.pallas_call(
        total_kernel,
        out_shape=jax.ShapeDtypeStruct((1,) + every.shape[2:], BF),
        in_specs=in_vmem(1),
        out_specs=pl.BlockSpec(memory_space=pltpu.VMEM),
        compiler_params=pltpu.CompilerParams(vmem_limit_bytes=2 << 20),
        name="total",
    )(every)


def body(queries, cache_keys, cache_values, new_keys, new_values, lengths, positions, out_weight):
    size = cache_keys.shape[3]
    slots = cache_keys.shape[2]
    rate = math.log2(math.e) / size**0.5
    n_ctx = lax.axis_size(CTX)
    here = lax.axis_index(CTX)
    info = jnp.stack([lengths[0] - here * slots, (here == 0).astype(jnp.int32)])
    mine = queries[0].reshape(1, -1, size)
    sent = jnp.broadcast_to(mine, (n_ctx,) + mine.shape[1:])
    q = lax.all_to_all(sent, CTX, 0, 0, tiled=True)
    staged = stage(cache_keys[0], cache_values[0], new_keys[0], new_values[0], positions)
    part = attend(info, q, *staged)
    part = lax.all_to_all(part, "x", 0, 0, tiled=True)
    part = combine(part, lax.axis_size(Z), False, rate)
    part = lax.all_to_all(part, Z, 0, 0, tiled=True)
    spread = ("x", "y", "zb")
    sizes = tuple(lax.axis_size(a) for a in spread)
    rows = combine(part, math.prod(sizes), True, rate)
    rows = lax.all_to_all(rows, spread, 0, 0, tiled=True)
    out = project(rows.reshape(*sizes, *rows.shape[1:]), out_weight)
    every = lax.all_gather(out, HEAD, axis=0)
    return total_of(every)


def solution(mesh):
    fine = Mesh(mesh.devices.reshape(4, 4, 2, 2, 2, 4), ("x", "za", "zb", "zh", "core", "y"))
    in_specs = (
        P("y", HEAD, CTX, None),
        P("y", HEAD, CTX, None),
        P("y", HEAD, CTX, None),
        P("y", HEAD, None, None),
        P("y", HEAD, None, None),
        P("y"),
        P("y", None),
        P(HEAD, CTX + ("y",)),
    )
    out_specs = P(HEAD, None, CTX + ("y",))
    return jax.shard_map(body, mesh=fine, in_specs=in_specs, out_specs=out_specs, check_vma=False)
```

```python
import functools
import math

import jax
import jax.numpy as jnp
from jax import lax
from jax.experimental import pallas as pl
from jax.experimental.pallas import tpu as pltpu
from jax.sharding import Mesh
from jax.sharding import PartitionSpec as P

NEW = 16
QPK = 16
NEG = -1e30
Z = ("za", "zb")
CTX = ("x",) + Z
HEAD = ("zh", "core")
BF = jnp.bfloat16
F32 = jnp.float32
STAT_ROWS = 16


def iota(shape, dim):
    return lax.broadcasted_iota(jnp.int32, shape, dim)


def dot_nt(a, b):
    return lax.dot_general(a, b, (((1,), (1,)), ((), ())), preferred_element_type=F32)


def split3(row):
    hi = row.astype(BF).astype(F32)
    rest = row - hi
    mid = rest.astype(BF).astype(F32)
    return hi, mid, rest - mid


def pack_stats(top, total):
    rows = split3(top) + split3(total)
    at = iota((STAT_ROWS, top.shape[1]), 0)
    out = jnp.zeros((STAT_ROWS, top.shape[1]), F32)
    for n, row in enumerate(rows):
        out = jnp.where(at == n, row, out)
    return out.astype(BF)


def unpack_stats(tile):
    rows = tile.astype(F32)
    top = (rows[0:1] + rows[1:2]) + rows[2:3]
    total = (rows[3:4] + rows[4:5]) + rows[5:6]
    return top, total


def attend_kernel(length, q_ref, keys, values, fresh_keys, fresh_values, pos_ref, out_ref, scores, *, rate, chunk):
    heads, slots, size = keys.shape
    rows = NEW * QPK
    here = lax.axis_index(CTX)
    valid = length[0] - here * slots
    half_rows = QPK // 2
    n = NEW * half_rows
    dest = iota((n, 1), 0)
    token = dest % NEW
    n_x = lax.axis_size("x")
    n_pairs = NEW // n_x
    source = (token % n_pairs * n_x + token // n_pairs) * half_rows + dest // NEW
    order = jnp.where(iota((n, n), 1) == source, 1.0, 0.0).astype(BF)
    arrived = q_ref[...].astype(F32).reshape(n_pairs, 2, n_x, heads * half_rows, size)

    def ordered(k, h):
        block = arrived[:, h, :, k * half_rows : (k + 1) * half_rows, :].reshape(n, size).astype(BF)
        return jnp.dot(order, block, preferred_element_type=F32).astype(BF)


    pos = jnp.broadcast_to(pos_ref[...], (rows, NEW))
    mine = jnp.where(iota((rows, NEW), 0) % NEW == iota((rows, NEW), 1), pos, 0)
    allow = jnp.logical_and(pos <= jnp.sum(mine, axis=1, keepdims=True), here == 0)

    def finish(k, acc, top):
        total = acc[:, size:]
        attended = (acc[:, :size] / total).astype(BF)
        for h in range(2):
            part_rows = slice(h * 128, (h + 1) * 128)
            lane = iota((128, 128), 1)
            cols = jnp.where(lane == 0, top[part_rows], total[part_rows])
            stats = jnp.transpose(cols)
            out_ref[2 * k + h, 0:128, :] = attended[part_rows]
            out_ref[2 * k + h, 128:, :] = pack_stats(stats[0:1], stats[1:2])

    tops = []
    for k in range(heads):
        q = jnp.concatenate([ordered(k, 0), ordered(k, 1)], axis=0)
        fresh = jnp.where(allow, dot_nt(q, fresh_keys[k]), NEG)
        part = jnp.full((rows, 128), NEG, F32)
        for c in range(slots // chunk):
            s = dot_nt(q, keys[k, pl.ds(c * chunk, chunk), :])
            s = jnp.where(iota((1, chunk), 1) + c * chunk < valid, s, NEG)
            scores[k, :, pl.ds(c * chunk, chunk)] = s
            for i in range(chunk // 128):
                part = jnp.maximum(part, s[:, i * 128 : (i + 1) * 128])
        top = jnp.maximum(jnp.max(part, axis=1, keepdims=True), jnp.max(fresh, axis=1, keepdims=True))
        tops.append((top, fresh))
    for k in range(heads):
        top, fresh = tops[k]
        weights = jnp.exp2((fresh - top) * rate).astype(BF)
        fresh_ones = jnp.concatenate([fresh_values[k], jnp.ones((NEW, size), BF)], axis=1)
        acc = jnp.dot(weights, fresh_ones, preferred_element_type=F32)
        for c in range(slots // chunk):
            w = jnp.exp2((scores[k, :, pl.ds(c * chunk, chunk)] - top) * rate).astype(BF)
            v = jnp.concatenate([values[k, pl.ds(c * chunk, chunk), :], jnp.ones((chunk, size), BF)], axis=1)
            acc = acc + jnp.dot(w, v, preferred_element_type=F32)
        finish(k, acc, top)


def combine_kernel(r_ref, out_ref, *, rate, last):
    sources = r_ref.shape[0]
    copies = out_ref.shape[0]
    rows = r_ref.shape[1] - STAT_ROWS
    size = r_ref.shape[2]
    stats = [unpack_stats(r_ref[s, rows:, :]) for s in range(sources)]
    top = functools.reduce(jnp.maximum, [m for m, _ in stats])
    weights = [t * jnp.exp2((m - top) * rate) for m, t in stats]
    total = functools.reduce(jnp.add, weights)
    at = iota((size, size), 0)
    factors = jnp.zeros((size, size), F32)
    for s in range(sources):
        factors = jnp.where(at == s, weights[s] / total, factors)
    factors = jnp.transpose(factors)
    out = jnp.zeros((rows, size), F32)
    for s in range(sources):
        out = out + factors[0:rows, s : s + 1] * r_ref[s, 0:rows, :].astype(F32)
    out = out.astype(BF)
    if last:
        for c in range(copies):
            out_ref[c] = out
        return
    half = rows // 2
    for h in range(2):
        if h:
            top, total = (jnp.concatenate([v[:, half:], v[:, :half]], axis=1) for v in (top, total))
        tail = pack_stats(top, total)
        for c in range(h, copies, 2):
            out_ref[c, 0:half, :] = out[h * half : (h + 1) * half]
            out_ref[c, half:, :] = tail


def project_kernel(r_ref, w_ref, out_ref):
    n_z, n_x, n_y, rows, size = r_ref.shape
    per = rows // NEW
    acc = jnp.zeros((n_y * NEW, w_ref.shape[1]), F32)
    for x in range(n_x):
        for z in range(n_z):
            for j in range(0, per, 2):
                block = jnp.concatenate(
                    [
                        jnp.concatenate([r_ref[z, x, y, pl.ds((j + i) * NEW, NEW), :] for y in range(n_y)], axis=0)
                        for i in range(2)
                    ],
                    axis=1,
                )
                start = ((x * n_z + z) * per + j) * size
                acc = acc + jnp.dot(block, w_ref[pl.ds(start, 2 * size), :], preferred_element_type=F32)
    out_ref[...] = acc.astype(BF).reshape(out_ref.shape)


def in_vmem(n):
    return [pl.BlockSpec(memory_space=pltpu.VMEM)] * n


def stage_kernel(*refs):
    count = (len(refs) - 1) // 2
    copies = [pltpu.make_async_copy(refs[n], refs[count + n], refs[-1].at[n]) for n in range(count)]
    for copy in copies:
        copy.start()
    for copy in copies:
        copy.wait()


def stage(*arrays):
    return pl.pallas_call(
        stage_kernel,
        out_shape=[jax.ShapeDtypeStruct(a.shape, a.dtype) for a in arrays],
        in_specs=[pl.BlockSpec(memory_space=pltpu.HBM)] * len(arrays),
        out_specs=in_vmem(len(arrays)),
        scratch_shapes=[pltpu.SemaphoreType.DMA((len(arrays),))],
        compiler_params=pltpu.CompilerParams(vmem_limit_bytes=8 << 20),
        cost_estimate=pl.CostEstimate(flops=0, bytes_accessed=2 * sum(a.size * 2 for a in arrays), transcendentals=0),
        name="stage",
    )(*[pltpu.with_memory_space_constraint(a, pltpu.HBM) for a in arrays])


def attend(length, q, keys, values, fresh_keys, fresh_values, pos):
    heads, slots, size = keys.shape
    rate = math.log2(math.e) / size**0.5
    chunk = min(slots, 256)
    flops = 4 * heads * NEW * QPK * slots * size
    return pl.pallas_call(
        functools.partial(attend_kernel, rate=rate, chunk=chunk),
        out_shape=jax.ShapeDtypeStruct((2 * heads, 128 + STAT_ROWS, size), BF),
        in_specs=[pl.BlockSpec(memory_space=pltpu.SMEM)] + in_vmem(6),
        out_specs=pl.BlockSpec(memory_space=pltpu.VMEM),
        scratch_shapes=[pltpu.VMEM((heads, NEW * QPK, slots), F32)],
        compiler_params=pltpu.CompilerParams(vmem_limit_bytes=13 << 20),
        cost_estimate=pl.CostEstimate(
            flops=flops, bytes_accessed=2 * heads * slots * size * 2, transcendentals=heads * NEW * QPK * slots
        ),
        name="attend",
    )(length, q, keys, values, fresh_keys, fresh_values, pos)


def combine(r, copies, last, rate):
    rows = r.shape[1] - STAT_ROWS if last else (r.shape[1] - STAT_ROWS) // 2 + STAT_ROWS
    return pl.pallas_call(
        functools.partial(combine_kernel, rate=rate, last=last),
        out_shape=jax.ShapeDtypeStruct((copies, rows, r.shape[2]), BF),
        in_specs=in_vmem(1),
        out_specs=pl.BlockSpec(memory_space=pltpu.VMEM),
        compiler_params=pltpu.CompilerParams(vmem_limit_bytes=8 << 20),
        name="combine_last" if last else "combine",
    )(r)


def project(r, w):
    return pl.pallas_call(
        project_kernel,
        out_shape=jax.ShapeDtypeStruct((r.shape[1], NEW, w.shape[1]), BF),
        in_specs=in_vmem(2),
        out_specs=pl.BlockSpec(memory_space=pltpu.VMEM),
        compiler_params=pltpu.CompilerParams(vmem_limit_bytes=8 << 20),
        name="project",
    )(r, w)


def total_kernel(every, out_ref):
    mine = lax.axis_index(HEAD)
    total = every[0, mine].astype(F32)
    for h in range(1, every.shape[0]):
        total = total + every[h, mine].astype(F32)
    out_ref[0] = total.astype(BF)


def total_of(every):
    return pl.pallas_call(
        total_kernel,
        out_shape=jax.ShapeDtypeStruct((1,) + every.shape[2:], BF),
        in_specs=in_vmem(1),
        out_specs=pl.BlockSpec(memory_space=pltpu.VMEM),
        compiler_params=pltpu.CompilerParams(vmem_limit_bytes=2 << 20),
        name="total",
    )(every)


def body(queries, cache_keys, cache_values, new_keys, new_values, lengths, positions, out_weight):
    size = cache_keys.shape[3]
    rate = math.log2(math.e) / size**0.5
    n_ctx = lax.axis_size(CTX)
    mine = queries[0].reshape(1, -1, size)
    sent = jnp.broadcast_to(mine, (n_ctx,) + mine.shape[1:])
    q = lax.all_to_all(sent, Z + ("x",), 0, 0, tiled=True)
    staged = stage(cache_keys[0], cache_values[0], new_keys[0], new_values[0], positions)
    part = attend(lengths, q, *staged)
    part = lax.all_to_all(part, "x", 0, 0, tiled=True)
    part = combine(part, lax.axis_size(Z), False, rate)
    part = lax.all_to_all(part, Z, 0, 0, tiled=True)
    spread = ("zb", "x", "y")
    sizes = tuple(lax.axis_size(a) for a in spread)
    rows = combine(part, math.prod(sizes), True, rate)
    rows = lax.all_to_all(rows, spread, 0, 0, tiled=True)
    out = project(rows.reshape(*sizes, *rows.shape[1:]), out_weight)
    every = lax.all_gather(out, HEAD, axis=0)
    return total_of(every)


def solution(mesh):
    fine = Mesh(mesh.devices.reshape(4, 4, 2, 2, 2, 4), ("x", "za", "zb", "zh", "core", "y"))
    in_specs = (
        P("y", HEAD, CTX, None),
        P("y", HEAD, CTX, None),
        P("y", HEAD, CTX, None),
        P("y", HEAD, None, None),
        P("y", HEAD, None, None),
        P("y"),
        P("y", None),
        P(HEAD, CTX + ("y",)),
    )
    out_specs = P(HEAD, None, CTX + ("y",))
    return jax.shard_map(body, mesh=fine, in_specs=in_specs, out_specs=out_specs, check_vma=False)
```

```python
import functools
import math

import jax
import jax.numpy as jnp
from jax import lax
from jax.experimental import pallas as pl
from jax.experimental.pallas import tpu as pltpu
from jax.sharding import Mesh
from jax.sharding import PartitionSpec as P

NEW = 16
QPK = 16
NEG = -1e30
Z = ("za", "zb")
CTX = ("x",) + Z
HEAD = ("zh", "core")
BF = jnp.bfloat16
F32 = jnp.float32
STAT_ROWS = 16


def iota(shape, dim):
    return lax.broadcasted_iota(jnp.int32, shape, dim)


def dot_nt(a, b):
    return lax.dot_general(a, b, (((1,), (1,)), ((), ())), preferred_element_type=F32)


def split3(row):
    hi = row.astype(BF).astype(F32)
    rest = row - hi
    mid = rest.astype(BF).astype(F32)
    return hi, mid, rest - mid


def pack_stats(top, total):
    rows = split3(top) + split3(total)
    at = iota((STAT_ROWS, top.shape[1]), 0)
    out = jnp.zeros((STAT_ROWS, top.shape[1]), F32)
    for n, row in enumerate(rows):
        out = jnp.where(at == n, row, out)
    return out.astype(BF)


def unpack_stats(tile):
    rows = tile.astype(F32)
    top = (rows[0:1] + rows[1:2]) + rows[2:3]
    total = (rows[3:4] + rows[4:5]) + rows[5:6]
    return top, total


def attend_kernel(length, q_ref, keys, values, fresh_keys, fresh_values, pos_ref, out_ref, scores, *, rate, chunk):
    heads, slots, size = keys.shape
    rows = NEW * QPK
    here = lax.axis_index(CTX)
    valid = length[0] - here * slots
    half_rows = QPK // 2
    n = NEW * half_rows
    dest = iota((n, 1), 0)
    token = dest % NEW
    n_x = lax.axis_size("x")
    n_pairs = NEW // n_x
    place = (token + n_pairs // 2) % n_pairs
    source = (place * n_x + token // n_pairs) * half_rows + dest // NEW
    order = jnp.where(iota((n, n), 1) == source, 1.0, 0.0).astype(BF)
    arrived = q_ref[...].astype(F32).reshape(n_pairs, 2, n_x, heads * half_rows, size)

    def ordered(k, h):
        block = arrived[:, h, :, k * half_rows : (k + 1) * half_rows, :].reshape(n, size).astype(BF)
        return jnp.dot(order, block, preferred_element_type=F32).astype(BF)


    pos = jnp.broadcast_to(pos_ref[...], (rows, NEW))
    mine = jnp.where(iota((rows, NEW), 0) % NEW == iota((rows, NEW), 1), pos, 0)
    allow = jnp.logical_and(pos <= jnp.sum(mine, axis=1, keepdims=True), here == 0)

    def finish(k, acc, top):
        total = acc[:, size:]
        attended = (acc[:, :size] / total).astype(BF)
        lane = iota((size, size), 1)
        half = size // 2
        for h in range(2):
            part_rows = slice(h * size, (h + 1) * size)
            stats = jnp.transpose(jnp.where(lane == 0, top[part_rows], total[part_rows]))
            row_top, row_total = stats[0:1], stats[1:2]
            for p in range(2):
                if p:
                    row_top, row_total = (jnp.concatenate([v[:, half:], v[:, :half]], axis=1) for v in (row_top, row_total))
                start = h * size + p * half
                out_ref[4 * k + 2 * h + p, 0:half, :] = attended[start : start + half]
                out_ref[4 * k + 2 * h + p, half:, :] = pack_stats(row_top, row_total)

    tops = []
    for k in range(heads):
        q = jnp.concatenate([ordered(k, 0), ordered(k, 1)], axis=0)
        fresh = jnp.where(allow, dot_nt(q, fresh_keys[k]), NEG)
        part = jnp.full((rows, 128), NEG, F32)
        for c in range(slots // chunk):
            s = dot_nt(q, keys[k, pl.ds(c * chunk, chunk), :])
            s = jnp.where(iota((1, chunk), 1) + c * chunk < valid, s, NEG)
            scores[k, :, pl.ds(c * chunk, chunk)] = s
            for i in range(chunk // 128):
                part = jnp.maximum(part, s[:, i * 128 : (i + 1) * 128])
        top = jnp.maximum(jnp.max(part, axis=1, keepdims=True), jnp.max(fresh, axis=1, keepdims=True))
        tops.append((top, fresh))
    for k in range(heads):
        top, fresh = tops[k]
        weights = jnp.exp2((fresh - top) * rate).astype(BF)
        fresh_ones = jnp.concatenate([fresh_values[k], jnp.ones((NEW, size), BF)], axis=1)
        acc = jnp.dot(weights, fresh_ones, preferred_element_type=F32)
        for c in range(slots // chunk):
            w = jnp.exp2((scores[k, :, pl.ds(c * chunk, chunk)] - top) * rate).astype(BF)
            v = jnp.concatenate([values[k, pl.ds(c * chunk, chunk), :], jnp.ones((chunk, size), BF)], axis=1)
            acc = acc + jnp.dot(w, v, preferred_element_type=F32)
        finish(k, acc, top)


def combine_kernel(r_ref, out_ref, *, rate, last):
    sources = r_ref.shape[0]
    copies = out_ref.shape[0]
    rows = r_ref.shape[1] - STAT_ROWS
    size = r_ref.shape[2]
    stats = [unpack_stats(r_ref[s, rows:, :]) for s in range(sources)]
    top = functools.reduce(jnp.maximum, [m for m, _ in stats])
    weights = [t * jnp.exp2((m - top) * rate) for m, t in stats]
    total = functools.reduce(jnp.add, weights)
    at = iota((size, size), 0)
    factors = jnp.zeros((size, size), F32)
    for s in range(sources):
        factors = jnp.where(at == s, weights[s] / total, factors)
    factors = jnp.transpose(factors)
    out = jnp.zeros((rows, size), F32)
    for s in range(sources):
        out = out + factors[0:rows, s : s + 1] * r_ref[s, 0:rows, :].astype(F32)
    out = out.astype(BF)
    tail = None if last else pack_stats(top, total)
    for c in range(copies):
        out_ref[c, 0:rows, :] = out
        if not last:
            out_ref[c, rows:, :] = tail


def project_kernel(r_ref, w_ref, out_ref):
    n_z, n_x, n_y, rows, size = r_ref.shape
    per = rows // NEW
    acc = jnp.zeros((n_y * NEW, w_ref.shape[1]), F32)
    for x in range(n_x):
        for z in range(n_z):
            for j in range(0, per, 2):
                block = jnp.concatenate(
                    [
                        jnp.concatenate([r_ref[z, x, y, pl.ds((j + i) * NEW, NEW), :] for y in range(n_y)], axis=0)
                        for i in range(2)
                    ],
                    axis=1,
                )
                start = ((x * n_z + z) * per + j) * size
                acc = acc + jnp.dot(block, w_ref[pl.ds(start, 2 * size), :], preferred_element_type=F32)
    out_ref[...] = acc.astype(BF).reshape(out_ref.shape)


def from_middle(count):
    return [[(n + count // 2) % count for n in range(count)]]


def in_vmem(n):
    return [pl.BlockSpec(memory_space=pltpu.VMEM)] * n


def stage_kernel(*refs):
    count = (len(refs) - 1) // 2
    copies = [pltpu.make_async_copy(refs[n], refs[count + n], refs[-1].at[n]) for n in range(count)]
    for copy in copies:
        copy.start()
    for copy in copies:
        copy.wait()


def stage(*arrays):
    return pl.pallas_call(
        stage_kernel,
        out_shape=[jax.ShapeDtypeStruct(a.shape, a.dtype) for a in arrays],
        in_specs=[pl.BlockSpec(memory_space=pltpu.HBM)] * len(arrays),
        out_specs=in_vmem(len(arrays)),
        scratch_shapes=[pltpu.SemaphoreType.DMA((len(arrays),))],
        compiler_params=pltpu.CompilerParams(vmem_limit_bytes=8 << 20),
        cost_estimate=pl.CostEstimate(flops=0, bytes_accessed=2 * sum(a.size * 2 for a in arrays), transcendentals=0),
        name="stage",
    )(*[pltpu.with_memory_space_constraint(a, pltpu.HBM) for a in arrays])


def attend(length, q, keys, values, fresh_keys, fresh_values, pos):
    heads, slots, size = keys.shape
    rate = math.log2(math.e) / size**0.5
    chunk = min(slots, 256)
    flops = 4 * heads * NEW * QPK * slots * size
    return pl.pallas_call(
        functools.partial(attend_kernel, rate=rate, chunk=chunk),
        out_shape=jax.ShapeDtypeStruct((4 * heads, size // 2 + STAT_ROWS, size), BF),
        in_specs=[pl.BlockSpec(memory_space=pltpu.SMEM)] + in_vmem(6),
        out_specs=pl.BlockSpec(memory_space=pltpu.VMEM),
        scratch_shapes=[pltpu.VMEM((heads, NEW * QPK, slots), F32)],
        compiler_params=pltpu.CompilerParams(vmem_limit_bytes=13 << 20),
        cost_estimate=pl.CostEstimate(
            flops=flops, bytes_accessed=2 * heads * slots * size * 2, transcendentals=heads * NEW * QPK * slots
        ),
        name="attend",
    )(length, q, keys, values, fresh_keys, fresh_values, pos)


def combine(r, copies, last, rate):
    rows = r.shape[1] - STAT_ROWS if last else r.shape[1]
    return pl.pallas_call(
        functools.partial(combine_kernel, rate=rate, last=last),
        out_shape=jax.ShapeDtypeStruct((copies, rows, r.shape[2]), BF),
        in_specs=in_vmem(1),
        out_specs=pl.BlockSpec(memory_space=pltpu.VMEM),
        compiler_params=pltpu.CompilerParams(vmem_limit_bytes=8 << 20),
        name="combine_last" if last else "combine",
    )(r)


def project(r, w):
    return pl.pallas_call(
        project_kernel,
        out_shape=jax.ShapeDtypeStruct((r.shape[1], NEW, w.shape[1]), BF),
        in_specs=in_vmem(2),
        out_specs=pl.BlockSpec(memory_space=pltpu.VMEM),
        compiler_params=pltpu.CompilerParams(vmem_limit_bytes=8 << 20),
        name="project",
    )(r, w)


def total_kernel(every, out_ref):
    mine = lax.axis_index(HEAD)
    total = every[0, mine].astype(F32)
    for h in range(1, every.shape[0]):
        total = total + every[h, mine].astype(F32)
    out_ref[0] = total.astype(BF)


def total_of(every):
    return pl.pallas_call(
        total_kernel,
        out_shape=jax.ShapeDtypeStruct((1,) + every.shape[2:], BF),
        in_specs=in_vmem(1),
        out_specs=pl.BlockSpec(memory_space=pltpu.VMEM),
        compiler_params=pltpu.CompilerParams(vmem_limit_bytes=2 << 20),
        name="total",
    )(every)


def body(queries, cache_keys, cache_values, new_keys, new_values, lengths, positions, out_weight):
    size = cache_keys.shape[3]
    rate = math.log2(math.e) / size**0.5
    n_ctx = lax.axis_size(CTX)
    mine = queries[0].reshape(1, -1, size)
    sent = jnp.broadcast_to(mine, (n_ctx,) + mine.shape[1:])
    q = lax.all_to_all(sent, Z + ("x",), 0, 0, axis_index_groups=from_middle(n_ctx), tiled=True)
    staged = stage(cache_keys[0], cache_values[0], new_keys[0], new_values[0], positions)
    part = attend(lengths, q, *staged)
    part = lax.all_to_all(part, ("x", "zb"), 0, 0, tiled=True)
    part = combine(part, lax.axis_size("za"), False, rate)
    part = lax.all_to_all(part, "za", 0, 0, axis_index_groups=from_middle(lax.axis_size("za")), tiled=True)
    spread = ("zb", "x", "y")
    sizes = tuple(lax.axis_size(a) for a in spread)
    rows = combine(part, math.prod(sizes), True, rate)
    rows = lax.all_to_all(rows, spread, 0, 0, tiled=True)
    out = project(rows.reshape(*sizes, *rows.shape[1:]), out_weight)
    every = lax.all_gather(out, HEAD, axis=0)
    return total_of(every)


def solution(mesh):
    fine = Mesh(mesh.devices.reshape(4, 4, 2, 2, 2, 4), ("x", "za", "zb", "zh", "core", "y"))
    in_specs = (
        P("y", HEAD, CTX, None),
        P("y", HEAD, CTX, None),
        P("y", HEAD, CTX, None),
        P("y", HEAD, None, None),
        P("y", HEAD, None, None),
        P("y"),
        P("y", None),
        P(HEAD, CTX + ("y",)),
    )
    out_specs = P(HEAD, None, CTX + ("y",))
    return jax.shard_map(body, mesh=fine, in_specs=in_specs, out_specs=out_specs, check_vma=False)
```

```python
import functools
import math

import jax
import jax.numpy as jnp
from jax import lax
from jax.experimental import pallas as pl
from jax.experimental.pallas import tpu as pltpu
from jax.sharding import Mesh
from jax.sharding import PartitionSpec as P

NEW = 16
QPK = 16
NEG = -1e30
Z = ("za", "zb")
CTX = ("x",) + Z
HEAD = ("zh", "core")
BF = jnp.bfloat16
F32 = jnp.float32
STAT_ROWS = 16


def iota(shape, dim):
    return lax.broadcasted_iota(jnp.int32, shape, dim)


def dot_nt(a, b):
    return lax.dot_general(a, b, (((1,), (1,)), ((), ())), preferred_element_type=F32)


def split3(row):
    hi = row.astype(BF).astype(F32)
    rest = row - hi
    mid = rest.astype(BF).astype(F32)
    return hi, mid, rest - mid


def pack_stats(top, total):
    rows = split3(top) + split3(total)
    at = iota((STAT_ROWS, top.shape[1]), 0)
    out = jnp.zeros((STAT_ROWS, top.shape[1]), F32)
    for n, row in enumerate(rows):
        out = jnp.where(at == n, row, out)
    return out.astype(BF)


def unpack_stats(tile):
    rows = tile.astype(F32)
    top = (rows[0:1] + rows[1:2]) + rows[2:3]
    total = (rows[3:4] + rows[4:5]) + rows[5:6]
    return top, total


def attend_kernel(length, q_ref, keys, values, fresh_keys, fresh_values, pos_ref, out_ref, scores, *, rate, chunk):
    heads, slots, size = keys.shape
    rows = NEW * QPK
    here = lax.axis_index(CTX)
    valid = length[0] - here * slots
    half_rows = QPK // 2
    n = NEW * half_rows
    dest = iota((n, 1), 0)
    token = dest % NEW
    n_x = lax.axis_size("x")
    n_pairs = NEW // n_x
    place = (token + n_pairs // 2) % n_pairs
    source = (place * n_x + n_x - 1 - token // n_pairs) * half_rows + dest // NEW
    order = jnp.where(iota((n, n), 1) == source, 1.0, 0.0).astype(BF)
    arrived = q_ref[...].astype(F32).reshape(n_pairs, 2, n_x, heads * half_rows, size)

    def ordered(k, h):
        block = arrived[:, 1 - h, :, k * half_rows : (k + 1) * half_rows, :].reshape(n, size).astype(BF)
        return jnp.dot(order, block, preferred_element_type=F32).astype(BF)


    pos = jnp.broadcast_to(pos_ref[...], (rows, NEW))
    mine = jnp.where(iota((rows, NEW), 0) % NEW == iota((rows, NEW), 1), pos, 0)
    allow = jnp.logical_and(pos <= jnp.sum(mine, axis=1, keepdims=True), here == 0)

    def finish(k, acc, top):
        total = acc[:, size:]
        attended = (acc[:, :size] / total).astype(BF)
        lane = iota((size, size), 1)
        half = size // 2
        for h in range(2):
            part_rows = slice(h * size, (h + 1) * size)
            stats = jnp.transpose(jnp.where(lane == 0, top[part_rows], total[part_rows]))
            row_top, row_total = stats[0:1], stats[1:2]
            first = out_ref.shape[0] - 2 * (2 * k + h + 1)
            for p in range(2):
                if p:
                    row_top, row_total = (jnp.concatenate([v[:, half:], v[:, :half]], axis=1) for v in (row_top, row_total))
                start = h * size + p * half
                out_ref[first + p, 0:half, :] = attended[start : start + half]
                out_ref[first + p, half:, :] = pack_stats(row_top, row_total)

    tops = []
    for k in range(heads):
        q = jnp.concatenate([ordered(k, 0), ordered(k, 1)], axis=0)
        fresh = jnp.where(allow, dot_nt(q, fresh_keys[k]), NEG)
        part = jnp.full((rows, 128), NEG, F32)
        for c in range(slots // chunk):
            s = dot_nt(q, keys[k, pl.ds(c * chunk, chunk), :])
            s = jnp.where(iota((1, chunk), 1) + c * chunk < valid, s, NEG)
            scores[k, :, pl.ds(c * chunk, chunk)] = s
            for i in range(chunk // 128):
                part = jnp.maximum(part, s[:, i * 128 : (i + 1) * 128])
        top = jnp.maximum(jnp.max(part, axis=1, keepdims=True), jnp.max(fresh, axis=1, keepdims=True))
        tops.append((top, fresh))
    for k in range(heads):
        top, fresh = tops[k]
        weights = jnp.exp2((fresh - top) * rate).astype(BF)
        fresh_ones = jnp.concatenate([fresh_values[k], jnp.ones((NEW, size), BF)], axis=1)
        acc = jnp.dot(weights, fresh_ones, preferred_element_type=F32)
        for c in range(slots // chunk):
            w = jnp.exp2((scores[k, :, pl.ds(c * chunk, chunk)] - top) * rate).astype(BF)
            v = jnp.concatenate([values[k, pl.ds(c * chunk, chunk), :], jnp.ones((chunk, size), BF)], axis=1)
            acc = acc + jnp.dot(w, v, preferred_element_type=F32)
        finish(k, acc, top)


def combine_kernel(r_ref, out_ref, *, rate, last):
    sources = r_ref.shape[0]
    copies = out_ref.shape[0]
    rows = r_ref.shape[1] - STAT_ROWS
    size = r_ref.shape[2]
    stats = [unpack_stats(r_ref[s, rows:, :]) for s in range(sources)]
    top = functools.reduce(jnp.maximum, [m for m, _ in stats])
    weights = [t * jnp.exp2((m - top) * rate) for m, t in stats]
    total = functools.reduce(jnp.add, weights)
    at = iota((size, size), 0)
    factors = jnp.zeros((size, size), F32)
    for s in range(sources):
        factors = jnp.where(at == s, weights[s] / total, factors)
    factors = jnp.transpose(factors)
    out = jnp.zeros((rows, size), F32)
    for s in range(sources):
        out = out + factors[0:rows, s : s + 1] * r_ref[s, 0:rows, :].astype(F32)
    out = out.astype(BF)
    tail = None if last else pack_stats(top, total)
    for c in range(copies):
        out_ref[c, 0:rows, :] = out
        if not last:
            out_ref[c, rows:, :] = tail


def project_kernel(r_ref, w_ref, out_ref):
    n_z, n_x, n_y, rows, size = r_ref.shape
    per = rows // NEW
    acc = jnp.zeros((n_y * NEW, w_ref.shape[1]), F32)
    for x in range(n_x):
        for z in range(n_z):
            for j in range(0, per, 2):
                block = jnp.concatenate(
                    [
                        jnp.concatenate([r_ref[z, n_x - 1 - x, n_y - 1 - y, pl.ds((j + i) * NEW, NEW), :] for y in range(n_y)], axis=0)
                        for i in range(2)
                    ],
                    axis=1,
                )
                start = ((x * n_z + z) * per + j) * size
                acc = acc + jnp.dot(block, w_ref[pl.ds(start, 2 * size), :], preferred_element_type=F32)
    out_ref[...] = acc.astype(BF).reshape(out_ref.shape)


def listed(count, flip):
    return [[n ^ flip for n in range(count)]]


def in_vmem(n):
    return [pl.BlockSpec(memory_space=pltpu.VMEM)] * n


def stage_kernel(*refs):
    count = (len(refs) - 1) // 2
    copies = [pltpu.make_async_copy(refs[n], refs[count + n], refs[-1].at[n]) for n in range(count)]
    for copy in copies:
        copy.start()
    for copy in copies:
        copy.wait()


def stage(*arrays):
    return pl.pallas_call(
        stage_kernel,
        out_shape=[jax.ShapeDtypeStruct(a.shape, a.dtype) for a in arrays],
        in_specs=[pl.BlockSpec(memory_space=pltpu.HBM)] * len(arrays),
        out_specs=in_vmem(len(arrays)),
        scratch_shapes=[pltpu.SemaphoreType.DMA((len(arrays),))],
        compiler_params=pltpu.CompilerParams(vmem_limit_bytes=8 << 20),
        cost_estimate=pl.CostEstimate(flops=0, bytes_accessed=2 * sum(a.size * 2 for a in arrays), transcendentals=0),
        name="stage",
    )(*[pltpu.with_memory_space_constraint(a, pltpu.HBM) for a in arrays])


def attend(length, q, keys, values, fresh_keys, fresh_values, pos):
    heads, slots, size = keys.shape
    rate = math.log2(math.e) / size**0.5
    chunk = min(slots, 256)
    flops = 4 * heads * NEW * QPK * slots * size
    return pl.pallas_call(
        functools.partial(attend_kernel, rate=rate, chunk=chunk),
        out_shape=jax.ShapeDtypeStruct((4 * heads, size // 2 + STAT_ROWS, size), BF),
        in_specs=[pl.BlockSpec(memory_space=pltpu.SMEM)] + in_vmem(6),
        out_specs=pl.BlockSpec(memory_space=pltpu.VMEM),
        scratch_shapes=[pltpu.VMEM((heads, NEW * QPK, slots), F32)],
        compiler_params=pltpu.CompilerParams(vmem_limit_bytes=13 << 20),
        cost_estimate=pl.CostEstimate(
            flops=flops, bytes_accessed=2 * heads * slots * size * 2, transcendentals=heads * NEW * QPK * slots
        ),
        name="attend",
    )(length, q, keys, values, fresh_keys, fresh_values, pos)


def combine(r, copies, last, rate):
    rows = r.shape[1] - STAT_ROWS if last else r.shape[1]
    return pl.pallas_call(
        functools.partial(combine_kernel, rate=rate, last=last),
        out_shape=jax.ShapeDtypeStruct((copies, rows, r.shape[2]), BF),
        in_specs=in_vmem(1),
        out_specs=pl.BlockSpec(memory_space=pltpu.VMEM),
        compiler_params=pltpu.CompilerParams(vmem_limit_bytes=8 << 20),
        name="combine_last" if last else "combine",
    )(r)


def project(r, w):
    return pl.pallas_call(
        project_kernel,
        out_shape=jax.ShapeDtypeStruct((r.shape[1], NEW, w.shape[1]), BF),
        in_specs=in_vmem(2),
        out_specs=pl.BlockSpec(memory_space=pltpu.VMEM),
        compiler_params=pltpu.CompilerParams(vmem_limit_bytes=8 << 20),
        name="project",
    )(r, w)


def total_kernel(every, out_ref):
    mine = lax.axis_index(HEAD)
    total = every[0, mine].astype(F32)
    for h in range(1, every.shape[0]):
        total = total + every[h, mine].astype(F32)
    out_ref[0] = total.astype(BF)


def total_of(every):
    return pl.pallas_call(
        total_kernel,
        out_shape=jax.ShapeDtypeStruct((1,) + every.shape[2:], BF),
        in_specs=in_vmem(1),
        out_specs=pl.BlockSpec(memory_space=pltpu.VMEM),
        compiler_params=pltpu.CompilerParams(vmem_limit_bytes=2 << 20),
        name="total",
    )(every)


def body(queries, cache_keys, cache_values, new_keys, new_values, lengths, positions, out_weight):
    size = cache_keys.shape[3]
    rate = math.log2(math.e) / size**0.5
    n_ctx = lax.axis_size(CTX)
    mine = queries[0].reshape(1, -1, size)
    sent = jnp.broadcast_to(mine, (n_ctx,) + mine.shape[1:])
    q = lax.all_to_all(sent, Z + ("x",), 0, 0, axis_index_groups=listed(n_ctx, 23), tiled=True)
    staged = stage(cache_keys[0], cache_values[0], new_keys[0], new_values[0], positions)
    part = attend(lengths, q, *staged)
    part = lax.all_to_all(part, ("x", "zb"), 0, 0, axis_index_groups=listed(part.shape[0], 6), tiled=True)
    part = combine(part, lax.axis_size("za"), False, rate)
    part = lax.all_to_all(part, "za", 0, 0, axis_index_groups=listed(part.shape[0], 2), tiled=True)
    spread = ("zb", "x", "y")
    sizes = tuple(lax.axis_size(a) for a in spread)
    rows = combine(part, math.prod(sizes), True, rate)
    rows = lax.all_to_all(rows, spread, 0, 0, axis_index_groups=listed(rows.shape[0], 15), tiled=True)
    out = project(rows.reshape(*sizes, *rows.shape[1:]), out_weight)
    every = lax.all_gather(out, HEAD, axis=0, axis_index_groups=listed(lax.axis_size(HEAD), 2))
    return total_of(every)


def solution(mesh):
    fine = Mesh(mesh.devices.reshape(4, 4, 2, 2, 2, 4), ("x", "za", "zb", "zh", "core", "y"))
    in_specs = (
        P("y", HEAD, CTX, None),
        P("y", HEAD, CTX, None),
        P("y", HEAD, CTX, None),
        P("y", HEAD, None, None),
        P("y", HEAD, None, None),
        P("y"),
        P("y", None),
        P(HEAD, CTX + ("y",)),
    )
    out_specs = P(HEAD, None, CTX + ("y",))
    return jax.shard_map(body, mesh=fine, in_specs=in_specs, out_specs=out_specs, check_vma=False)
```

```python
import functools
import math

import jax
import jax.numpy as jnp
from jax import lax
from jax.experimental import pallas as pl
from jax.experimental.pallas import tpu as pltpu
from jax.sharding import Mesh
from jax.sharding import PartitionSpec as P

NEW = 16
QPK = 16
NEG = -1e30
Z = ("za", "zb")
CTX = ("x",) + Z
HEAD = ("zh", "core")
BF = jnp.bfloat16
F32 = jnp.float32
STAT_ROWS = 16


def iota(shape, dim):
    return lax.broadcasted_iota(jnp.int32, shape, dim)


def dot_nt(a, b):
    return lax.dot_general(a, b, (((1,), (1,)), ((), ())), preferred_element_type=F32)


def split3(row):
    hi = row.astype(BF).astype(F32)
    rest = row - hi
    mid = rest.astype(BF).astype(F32)
    return hi, mid, rest - mid


def pack_stats(top, total):
    rows = split3(top) + split3(total)
    at = iota((STAT_ROWS, top.shape[1]), 0)
    out = jnp.zeros((STAT_ROWS, top.shape[1]), F32)
    for n, row in enumerate(rows):
        out = jnp.where(at == n, row, out)
    return out.astype(BF)


def unpack_stats(tile):
    rows = tile.astype(F32)
    top = (rows[0:1] + rows[1:2]) + rows[2:3]
    total = (rows[3:4] + rows[4:5]) + rows[5:6]
    return top, total


def attend_kernel(length, q_ref, keys, values, fresh_keys, fresh_values, pos_ref, out_ref, scores, *, rate, chunk):
    heads, slots, size = keys.shape
    rows = NEW * QPK
    here = lax.axis_index(CTX)
    valid = length[0] - here * slots
    half_rows = QPK // 2
    n = NEW * half_rows
    dest = iota((n, 1), 0)
    token = dest % NEW
    n_x = lax.axis_size("x")
    n_pairs = NEW // n_x
    place = (token + n_pairs // 2) % n_pairs
    source = (place * n_x + n_x - 1 - token // n_pairs) * half_rows + dest // NEW
    order = jnp.where(iota((n, n), 1) == source, 1.0, 0.0).astype(BF)
    arrived = q_ref[...].astype(F32).reshape(n_pairs, 2, n_x, heads * half_rows, size)

    def ordered(k, h):
        block = arrived[:, 1 - h, :, k * half_rows : (k + 1) * half_rows, :].reshape(n, size).astype(BF)
        return jnp.dot(order, block, preferred_element_type=F32).astype(BF)


    pos = jnp.broadcast_to(pos_ref[...], (rows, NEW))
    mine = jnp.where(iota((rows, NEW), 0) % NEW == iota((rows, NEW), 1), pos, 0)
    allow = jnp.logical_and(pos <= jnp.sum(mine, axis=1, keepdims=True), here == 0)

    def finish(k, acc, top):
        total = acc[:, size:]
        attended = (acc[:, :size] / total).astype(BF)
        lane = iota((size, size), 1)
        half = size // 2
        for h in range(2):
            part_rows = slice(h * size, (h + 1) * size)
            stats = jnp.transpose(jnp.where(lane == 0, top[part_rows], total[part_rows]))
            row_top, row_total = stats[0:1], stats[1:2]
            quarters = out_ref.shape[0] // 2
            first = quarters - 1 - (2 * k + h)
            for p in range(2):
                if p:
                    row_top, row_total = (jnp.concatenate([v[:, half:], v[:, :half]], axis=1) for v in (row_top, row_total))
                start = h * size + p * half
                out_ref[p * quarters + first, 0:half, :] = attended[start : start + half]
                out_ref[p * quarters + first, half:, :] = pack_stats(row_top, row_total)

    tops = []
    for k in range(heads):
        q = jnp.concatenate([ordered(k, 0), ordered(k, 1)], axis=0)
        fresh = jnp.where(allow, dot_nt(q, fresh_keys[k]), NEG)
        part = jnp.full((rows, 128), NEG, F32)
        for c in range(slots // chunk):
            s = dot_nt(q, keys[k, pl.ds(c * chunk, chunk), :])
            s = jnp.where(iota((1, chunk), 1) + c * chunk < valid, s, NEG)
            scores[k, :, pl.ds(c * chunk, chunk)] = s
            for i in range(chunk // 128):
                part = jnp.maximum(part, s[:, i * 128 : (i + 1) * 128])
        top = jnp.maximum(jnp.max(part, axis=1, keepdims=True), jnp.max(fresh, axis=1, keepdims=True))
        tops.append((top, fresh))
    for k in range(heads):
        top, fresh = tops[k]
        weights = jnp.exp2((fresh - top) * rate).astype(BF)
        fresh_ones = jnp.concatenate([fresh_values[k], jnp.ones((NEW, size), BF)], axis=1)
        acc = jnp.dot(weights, fresh_ones, preferred_element_type=F32)
        for c in range(slots // chunk):
            w = jnp.exp2((scores[k, :, pl.ds(c * chunk, chunk)] - top) * rate).astype(BF)
            v = jnp.concatenate([values[k, pl.ds(c * chunk, chunk), :], jnp.ones((chunk, size), BF)], axis=1)
            acc = acc + jnp.dot(w, v, preferred_element_type=F32)
        finish(k, acc, top)


def combine_kernel(r_ref, out_ref, *, rate, last):
    sources = r_ref.shape[0]
    copies = out_ref.shape[0]
    rows = r_ref.shape[1] - STAT_ROWS
    size = r_ref.shape[2]
    stats = [unpack_stats(r_ref[s, rows:, :]) for s in range(sources)]
    top = functools.reduce(jnp.maximum, [m for m, _ in stats])
    weights = [t * jnp.exp2((m - top) * rate) for m, t in stats]
    total = functools.reduce(jnp.add, weights)
    at = iota((size, size), 0)
    factors = jnp.zeros((size, size), F32)
    for s in range(sources):
        factors = jnp.where(at == s, weights[s] / total, factors)
    factors = jnp.transpose(factors)
    out = jnp.zeros((rows, size), F32)
    for s in range(sources):
        out = out + factors[0:rows, s : s + 1] * r_ref[s, 0:rows, :].astype(F32)
    out = out.astype(BF)
    tail = None if last else pack_stats(top, total)
    for c in range(copies):
        out_ref[c, 0:rows, :] = out
        if not last:
            out_ref[c, rows:, :] = tail


def project_kernel(r_ref, w_ref, out_ref):
    n_z, n_x, n_y, rows, size = r_ref.shape
    per = rows // NEW
    acc = jnp.zeros((n_y * NEW, w_ref.shape[1]), F32)
    for x in range(n_x):
        for z in range(n_z):
            for j in range(0, per, 2):
                block = jnp.concatenate(
                    [
                        jnp.concatenate([r_ref[z, (x + n_x // 2) % n_x, (y + n_y // 2) % n_y, pl.ds((j + i) * NEW, NEW), :] for y in range(n_y)], axis=0)
                        for i in range(2)
                    ],
                    axis=1,
                )
                start = ((x * n_z + z) * per + j) * size
                acc = acc + jnp.dot(block, w_ref[pl.ds(start, 2 * size), :], preferred_element_type=F32)
    out_ref[...] = acc.astype(BF).reshape(out_ref.shape)


def listed(count, flip):
    return [[n ^ flip for n in range(count)]]


def in_vmem(n):
    return [pl.BlockSpec(memory_space=pltpu.VMEM)] * n


def stage_kernel(*refs):
    count = (len(refs) - 1) // 2
    copies = [pltpu.make_async_copy(refs[n], refs[count + n], refs[-1].at[n]) for n in range(count)]
    for copy in copies:
        copy.start()
    for copy in copies:
        copy.wait()


def stage(*arrays):
    return pl.pallas_call(
        stage_kernel,
        out_shape=[jax.ShapeDtypeStruct(a.shape, a.dtype) for a in arrays],
        in_specs=[pl.BlockSpec(memory_space=pltpu.HBM)] * len(arrays),
        out_specs=in_vmem(len(arrays)),
        scratch_shapes=[pltpu.SemaphoreType.DMA((len(arrays),))],
        compiler_params=pltpu.CompilerParams(vmem_limit_bytes=8 << 20),
        cost_estimate=pl.CostEstimate(flops=0, bytes_accessed=2 * sum(a.size * 2 for a in arrays), transcendentals=0),
        name="stage",
    )(*[pltpu.with_memory_space_constraint(a, pltpu.HBM) for a in arrays])


def attend(length, q, keys, values, fresh_keys, fresh_values, pos):
    heads, slots, size = keys.shape
    rate = math.log2(math.e) / size**0.5
    chunk = min(slots, 256)
    flops = 4 * heads * NEW * QPK * slots * size
    return pl.pallas_call(
        functools.partial(attend_kernel, rate=rate, chunk=chunk),
        out_shape=jax.ShapeDtypeStruct((4 * heads, size // 2 + STAT_ROWS, size), BF),
        in_specs=[pl.BlockSpec(memory_space=pltpu.SMEM)] + in_vmem(6),
        out_specs=pl.BlockSpec(memory_space=pltpu.VMEM),
        scratch_shapes=[pltpu.VMEM((heads, NEW * QPK, slots), F32)],
        compiler_params=pltpu.CompilerParams(vmem_limit_bytes=13 << 20),
        cost_estimate=pl.CostEstimate(
            flops=flops, bytes_accessed=2 * heads * slots * size * 2, transcendentals=heads * NEW * QPK * slots
        ),
        name="attend",
    )(length, q, keys, values, fresh_keys, fresh_values, pos)


def combine(r, copies, last, rate):
    rows = r.shape[1] - STAT_ROWS if last else r.shape[1]
    return pl.pallas_call(
        functools.partial(combine_kernel, rate=rate, last=last),
        out_shape=jax.ShapeDtypeStruct((copies, rows, r.shape[2]), BF),
        in_specs=in_vmem(1),
        out_specs=pl.BlockSpec(memory_space=pltpu.VMEM),
        compiler_params=pltpu.CompilerParams(vmem_limit_bytes=8 << 20),
        name="combine_last" if last else "combine",
    )(r)


def project(r, w):
    return pl.pallas_call(
        project_kernel,
        out_shape=jax.ShapeDtypeStruct((r.shape[1], NEW, w.shape[1]), BF),
        in_specs=in_vmem(2),
        out_specs=pl.BlockSpec(memory_space=pltpu.VMEM),
        compiler_params=pltpu.CompilerParams(vmem_limit_bytes=8 << 20),
        name="project",
    )(r, w)


def total_kernel(every, out_ref):
    mine = lax.axis_index(HEAD)
    total = every[0, mine].astype(F32)
    for h in range(1, every.shape[0]):
        total = total + every[h, mine].astype(F32)
    out_ref[0] = total.astype(BF)


def total_of(every):
    return pl.pallas_call(
        total_kernel,
        out_shape=jax.ShapeDtypeStruct((1,) + every.shape[2:], BF),
        in_specs=in_vmem(1),
        out_specs=pl.BlockSpec(memory_space=pltpu.VMEM),
        compiler_params=pltpu.CompilerParams(vmem_limit_bytes=2 << 20),
        name="total",
    )(every)


def body(queries, cache_keys, cache_values, new_keys, new_values, lengths, positions, out_weight):
    size = cache_keys.shape[3]
    rate = math.log2(math.e) / size**0.5
    n_ctx = lax.axis_size(CTX)
    mine = queries[0].reshape(1, -1, size)
    sent = jnp.broadcast_to(mine, (n_ctx,) + mine.shape[1:])
    q = lax.all_to_all(sent, Z + ("x",), 0, 0, axis_index_groups=listed(n_ctx, 23), tiled=True)
    staged = stage(cache_keys[0], cache_values[0], new_keys[0], new_values[0], positions)
    part = attend(lengths, q, *staged)
    part = lax.all_to_all(part, ("zb", "x"), 0, 0, axis_index_groups=listed(part.shape[0], 3), tiled=True)
    part = combine(part, lax.axis_size("za"), False, rate)
    part = lax.all_to_all(part, "za", 0, 0, axis_index_groups=listed(part.shape[0], 2), tiled=True)
    spread = ("zb", "x", "y")
    sizes = tuple(lax.axis_size(a) for a in spread)
    rows = combine(part, math.prod(sizes), True, rate)
    rows = lax.all_to_all(rows, spread, 0, 0, axis_index_groups=listed(rows.shape[0], 10), tiled=True)
    out = project(rows.reshape(*sizes, *rows.shape[1:]), out_weight)
    every = lax.all_gather(out, HEAD, axis=0, axis_index_groups=listed(lax.axis_size(HEAD), 2))
    return total_of(every)


def solution(mesh):
    fine = Mesh(mesh.devices.reshape(4, 4, 2, 2, 2, 4), ("x", "za", "zb", "zh", "core", "y"))
    in_specs = (
        P("y", HEAD, CTX, None),
        P("y", HEAD, CTX, None),
        P("y", HEAD, CTX, None),
        P("y", HEAD, None, None),
        P("y", HEAD, None, None),
        P("y"),
        P("y", None),
        P(HEAD, CTX + ("y",)),
    )
    out_specs = P(HEAD, None, CTX + ("y",))
    return jax.shard_map(body, mesh=fine, in_specs=in_specs, out_specs=out_specs, check_vma=False)
```

```python
import functools
import math

import jax
import jax.numpy as jnp
from jax import lax
from jax.experimental import pallas as pl
from jax.experimental.pallas import tpu as pltpu
from jax.sharding import Mesh
from jax.sharding import PartitionSpec as P

NEW = 16
QPK = 16
NEG = -1e30
Z = ("za", "zb")
CTX = ("x",) + Z
HEAD = ("zh", "core")
BF = jnp.bfloat16
F32 = jnp.float32
STAT_ROWS = 16


def iota(shape, dim):
    return lax.broadcasted_iota(jnp.int32, shape, dim)


def dot_nt(a, b):
    return lax.dot_general(a, b, (((1,), (1,)), ((), ())), preferred_element_type=F32)


def split3(row):
    hi = row.astype(BF).astype(F32)
    rest = row - hi
    mid = rest.astype(BF).astype(F32)
    return hi, mid, rest - mid


def pack_stats(top, total):
    rows = split3(top) + split3(total)
    at = iota((STAT_ROWS, top.shape[1]), 0)
    out = jnp.zeros((STAT_ROWS, top.shape[1]), F32)
    for n, row in enumerate(rows):
        out = jnp.where(at == n, row, out)
    return out.astype(BF)


def unpack_stats(tile):
    rows = tile.astype(F32)
    top = (rows[0:1] + rows[1:2]) + rows[2:3]
    total = (rows[3:4] + rows[4:5]) + rows[5:6]
    return top, total


def attend_kernel(length, q_ref, keys, values, fresh_keys, fresh_values, pos_ref, out_ref, scores, *, rate, chunk):
    heads, slots, size = keys.shape
    rows = NEW * QPK
    here = lax.axis_index(CTX)
    valid = length[0] - here * slots
    half_rows = QPK // 2
    n = NEW * half_rows
    dest = iota((n, 1), 0)
    token = dest % NEW
    n_x = lax.axis_size("x")
    n_pairs = NEW // n_x
    place = (token + n_pairs // 2) % n_pairs
    source = (place * n_x + (token // n_pairs + n_x // 2) % n_x) * half_rows + dest // NEW
    order = jnp.where(iota((n, n), 1) == source, 1.0, 0.0).astype(BF)
    arrived = q_ref[...].astype(F32).reshape(n_pairs, 2, n_x, heads * half_rows, size)

    def ordered(k, h):
        block = arrived[:, 1 - h, :, k * half_rows : (k + 1) * half_rows, :].reshape(n, size).astype(BF)
        return jnp.dot(order, block, preferred_element_type=F32).astype(BF)


    pos = jnp.broadcast_to(pos_ref[...], (rows, NEW))
    mine = jnp.where(iota((rows, NEW), 0) % NEW == iota((rows, NEW), 1), pos, 0)
    allow = jnp.logical_and(pos <= jnp.sum(mine, axis=1, keepdims=True), here == 0)

    def finish(k, acc, top):
        total = acc[:, size:]
        attended = (acc[:, :size] / total).astype(BF)
        lane = iota((size, size), 1)
        half = size // 2
        for h in range(2):
            part_rows = slice(h * size, (h + 1) * size)
            stats = jnp.transpose(jnp.where(lane == 0, top[part_rows], total[part_rows]))
            row_top, row_total = stats[0:1], stats[1:2]
            quarters = out_ref.shape[0] // 2
            first = (2 * k + h + quarters // 2) % quarters
            for p in range(2):
                if p:
                    row_top, row_total = (jnp.concatenate([v[:, half:], v[:, :half]], axis=1) for v in (row_top, row_total))
                start = h * size + p * half
                out_ref[p * quarters + first, 0:half, :] = attended[start : start + half]
                out_ref[p * quarters + first, half:, :] = pack_stats(row_top, row_total)

    tops = []
    for k in range(heads):
        q = jnp.concatenate([ordered(k, 0), ordered(k, 1)], axis=0)
        fresh = jnp.where(allow, dot_nt(q, fresh_keys[k]), NEG)
        part = jnp.full((rows, 128), NEG, F32)
        for c in range(slots // chunk):
            s = dot_nt(q, keys[k, pl.ds(c * chunk, chunk), :])
            s = jnp.where(iota((1, chunk), 1) + c * chunk < valid, s, NEG)
            scores[k, :, pl.ds(c * chunk, chunk)] = s
            for i in range(chunk // 128):
                part = jnp.maximum(part, s[:, i * 128 : (i + 1) * 128])
        top = jnp.maximum(jnp.max(part, axis=1, keepdims=True), jnp.max(fresh, axis=1, keepdims=True))
        tops.append((top, fresh))
    for k in range(heads):
        top, fresh = tops[k]
        weights = jnp.exp2((fresh - top) * rate).astype(BF)
        fresh_ones = jnp.concatenate([fresh_values[k], jnp.ones((NEW, size), BF)], axis=1)
        acc = jnp.dot(weights, fresh_ones, preferred_element_type=F32)
        for c in range(slots // chunk):
            w = jnp.exp2((scores[k, :, pl.ds(c * chunk, chunk)] - top) * rate).astype(BF)
            v = jnp.concatenate([values[k, pl.ds(c * chunk, chunk), :], jnp.ones((chunk, size), BF)], axis=1)
            acc = acc + jnp.dot(w, v, preferred_element_type=F32)
        finish(k, acc, top)


def combine_kernel(r_ref, out_ref, *, rate, last):
    sources = r_ref.shape[0]
    copies = out_ref.shape[0]
    rows = r_ref.shape[1] - STAT_ROWS
    size = r_ref.shape[2]
    stats = [unpack_stats(r_ref[s, rows:, :]) for s in range(sources)]
    top = functools.reduce(jnp.maximum, [m for m, _ in stats])
    weights = [t * jnp.exp2((m - top) * rate) for m, t in stats]
    total = functools.reduce(jnp.add, weights)
    at = iota((size, size), 0)
    factors = jnp.zeros((size, size), F32)
    for s in range(sources):
        factors = jnp.where(at == s, weights[s] / total, factors)
    factors = jnp.transpose(factors)
    out = jnp.zeros((rows, size), F32)
    for s in range(sources):
        out = out + factors[0:rows, s : s + 1] * r_ref[s, 0:rows, :].astype(F32)
    out = out.astype(BF)
    tail = None if last else pack_stats(top, total)
    for c in range(copies):
        out_ref[c, 0:rows, :] = out
        if not last:
            out_ref[c, rows:, :] = tail


def project_kernel(r_ref, w_ref, out_ref):
    n_z, n_x, n_y, rows, size = r_ref.shape
    per = rows // NEW
    acc = jnp.zeros((n_y * NEW, w_ref.shape[1]), F32)
    for x in range(n_x):
        for z in range(n_z):
            for j in range(0, per, 2):
                block = jnp.concatenate(
                    [
                        jnp.concatenate([r_ref[z, (x + n_x // 2) % n_x, (y + n_y // 2) % n_y, pl.ds((j + i) * NEW, NEW), :] for y in range(n_y)], axis=0)
                        for i in range(2)
                    ],
                    axis=1,
                )
                start = ((x * n_z + z) * per + j) * size
                acc = acc + jnp.dot(block, w_ref[pl.ds(start, 2 * size), :], preferred_element_type=F32)
    out_ref[...] = acc.astype(BF).reshape(out_ref.shape)


def listed(count, flip):
    return [[n ^ flip for n in range(count)]]


def in_vmem(n):
    return [pl.BlockSpec(memory_space=pltpu.VMEM)] * n


def stage_kernel(*refs):
    count = (len(refs) - 1) // 2
    copies = [pltpu.make_async_copy(refs[n], refs[count + n], refs[-1].at[n]) for n in range(count)]
    for copy in copies:
        copy.start()
    for copy in copies:
        copy.wait()


def stage(*arrays):
    return pl.pallas_call(
        stage_kernel,
        out_shape=[jax.ShapeDtypeStruct(a.shape, a.dtype) for a in arrays],
        in_specs=[pl.BlockSpec(memory_space=pltpu.HBM)] * len(arrays),
        out_specs=in_vmem(len(arrays)),
        scratch_shapes=[pltpu.SemaphoreType.DMA((len(arrays),))],
        compiler_params=pltpu.CompilerParams(vmem_limit_bytes=8 << 20),
        cost_estimate=pl.CostEstimate(flops=0, bytes_accessed=2 * sum(a.size * 2 for a in arrays), transcendentals=0),
        name="stage",
    )(*[pltpu.with_memory_space_constraint(a, pltpu.HBM) for a in arrays])


def attend(length, q, keys, values, fresh_keys, fresh_values, pos):
    heads, slots, size = keys.shape
    rate = math.log2(math.e) / size**0.5
    chunk = min(slots, 256)
    flops = 4 * heads * NEW * QPK * slots * size
    return pl.pallas_call(
        functools.partial(attend_kernel, rate=rate, chunk=chunk),
        out_shape=jax.ShapeDtypeStruct((4 * heads, size // 2 + STAT_ROWS, size), BF),
        in_specs=[pl.BlockSpec(memory_space=pltpu.SMEM)] + in_vmem(6),
        out_specs=pl.BlockSpec(memory_space=pltpu.VMEM),
        scratch_shapes=[pltpu.VMEM((heads, NEW * QPK, slots), F32)],
        compiler_params=pltpu.CompilerParams(vmem_limit_bytes=13 << 20),
        cost_estimate=pl.CostEstimate(
            flops=flops, bytes_accessed=2 * heads * slots * size * 2, transcendentals=heads * NEW * QPK * slots
        ),
        name="attend",
    )(length, q, keys, values, fresh_keys, fresh_values, pos)


def combine(r, copies, last, rate):
    rows = r.shape[1] - STAT_ROWS if last else r.shape[1]
    return pl.pallas_call(
        functools.partial(combine_kernel, rate=rate, last=last),
        out_shape=jax.ShapeDtypeStruct((copies, rows, r.shape[2]), BF),
        in_specs=in_vmem(1),
        out_specs=pl.BlockSpec(memory_space=pltpu.VMEM),
        compiler_params=pltpu.CompilerParams(vmem_limit_bytes=8 << 20),
        name="combine_last" if last else "combine",
    )(r)


def project(r, w):
    return pl.pallas_call(
        project_kernel,
        out_shape=jax.ShapeDtypeStruct((r.shape[1], NEW, w.shape[1]), BF),
        in_specs=in_vmem(2),
        out_specs=pl.BlockSpec(memory_space=pltpu.VMEM),
        compiler_params=pltpu.CompilerParams(vmem_limit_bytes=8 << 20),
        name="project",
    )(r, w)


def total_kernel(every, out_ref):
    mine = lax.axis_index(HEAD)
    total = every[0, mine].astype(F32)
    for h in range(1, every.shape[0]):
        total = total + every[h, mine].astype(F32)
    out_ref[0] = total.astype(BF)


def total_of(every):
    return pl.pallas_call(
        total_kernel,
        out_shape=jax.ShapeDtypeStruct((1,) + every.shape[2:], BF),
        in_specs=in_vmem(1),
        out_specs=pl.BlockSpec(memory_space=pltpu.VMEM),
        compiler_params=pltpu.CompilerParams(vmem_limit_bytes=2 << 20),
        name="total",
    )(every)


def body(queries, cache_keys, cache_values, new_keys, new_values, lengths, positions, out_weight):
    size = cache_keys.shape[3]
    rate = math.log2(math.e) / size**0.5
    n_ctx = lax.axis_size(CTX)
    mine = queries[0].reshape(1, -1, size)
    sent = jnp.broadcast_to(mine, (n_ctx,) + mine.shape[1:])
    q = lax.all_to_all(sent, Z + ("x",), 0, 0, axis_index_groups=listed(n_ctx, 22), tiled=True)
    staged = stage(cache_keys[0], cache_values[0], new_keys[0], new_values[0], positions)
    part = attend(lengths, q, *staged)
    part = lax.all_to_all(part, ("zb", "x"), 0, 0, axis_index_groups=listed(part.shape[0], 2), tiled=True)
    part = combine(part, lax.axis_size("za"), False, rate)
    part = lax.all_to_all(part, "za", 0, 0, axis_index_groups=listed(part.shape[0], 2), tiled=True)
    spread = ("zb", "x", "y")
    sizes = tuple(lax.axis_size(a) for a in spread)
    rows = combine(part, math.prod(sizes), True, rate)
    rows = lax.all_to_all(rows, spread, 0, 0, axis_index_groups=listed(rows.shape[0], 10), tiled=True)
    out = project(rows.reshape(*sizes, *rows.shape[1:]), out_weight)
    every = lax.all_gather(out, HEAD, axis=0, axis_index_groups=listed(lax.axis_size(HEAD), 2))
    return total_of(every)


def solution(mesh):
    fine = Mesh(mesh.devices.reshape(4, 4, 2, 2, 2, 4), ("x", "za", "zb", "zh", "core", "y"))
    in_specs = (
        P("y", HEAD, CTX, None),
        P("y", HEAD, CTX, None),
        P("y", HEAD, CTX, None),
        P("y", HEAD, None, None),
        P("y", HEAD, None, None),
        P("y"),
        P("y", None),
        P(HEAD, CTX + ("y",)),
    )
    out_specs = P(HEAD, None, CTX + ("y",))
    return jax.shard_map(body, mesh=fine, in_specs=in_specs, out_specs=out_specs, check_vma=False)
```

```python
import functools
import math

import jax
import jax.numpy as jnp
from jax import lax
from jax.experimental import pallas as pl
from jax.experimental.pallas import tpu as pltpu
from jax.sharding import Mesh
from jax.sharding import PartitionSpec as P

NEW = 16
QPK = 16
NEG = -1e30
Z = ("za", "zb")
CTX = ("x",) + Z
HEAD = ("zh", "core")
BF = jnp.bfloat16
F32 = jnp.float32
STAT_ROWS = 16


def iota(shape, dim):
    return lax.broadcasted_iota(jnp.int32, shape, dim)


def dot_nt(a, b):
    return lax.dot_general(a, b, (((1,), (1,)), ((), ())), preferred_element_type=F32)


def split3(row):
    hi = row.astype(BF).astype(F32)
    rest = row - hi
    mid = rest.astype(BF).astype(F32)
    return hi, mid, rest - mid


def pack_stats(top, total):
    rows = split3(top) + split3(total)
    at = iota((STAT_ROWS, top.shape[1]), 0)
    out = jnp.zeros((STAT_ROWS, top.shape[1]), F32)
    for n, row in enumerate(rows):
        out = jnp.where(at == n, row, out)
    return out.astype(BF)


def unpack_stats(tile):
    rows = tile.astype(F32)
    top = (rows[0:1] + rows[1:2]) + rows[2:3]
    total = (rows[3:4] + rows[4:5]) + rows[5:6]
    return top, total


def attend_kernel(length, q_ref, keys, values, fresh_keys, fresh_values, pos_ref, out_ref, scores, *, rate, chunk):
    heads, slots, size = keys.shape
    rows = NEW * QPK
    here = lax.axis_index(CTX)
    valid = length[0] - here * slots
    half_rows = QPK // 2
    n = NEW * half_rows
    dest = iota((n, 1), 0)
    token = dest % NEW
    n_x = lax.axis_size("x")
    n_pairs = NEW // n_x
    place = (token + n_pairs // 2) % n_pairs
    source = (place * n_x + (token // n_pairs + n_x // 2) % n_x) * half_rows + dest // NEW
    order = jnp.where(iota((n, n), 1) == source, 1.0, 0.0).astype(BF)
    arrived = q_ref[...].astype(F32).reshape(n_pairs, 2, n_x, heads * half_rows, size)

    def ordered(k, h):
        block = arrived[:, 1 - h, :, k * half_rows : (k + 1) * half_rows, :].reshape(n, size).astype(BF)
        return jnp.dot(order, block, preferred_element_type=F32).astype(BF)


    pos = jnp.broadcast_to(pos_ref[...], (rows, NEW))
    mine = jnp.where(iota((rows, NEW), 0) % NEW == iota((rows, NEW), 1), pos, 0)
    allow = jnp.logical_and(pos <= jnp.sum(mine, axis=1, keepdims=True), here == 0)

    def finish(k, acc, top):
        total = acc[:, size:]
        attended = (acc[:, :size] / total).astype(BF)
        lane = iota((size, size), 1)
        half = size // 2
        for h in range(2):
            part_rows = slice(h * size, (h + 1) * size)
            stats = jnp.transpose(jnp.where(lane == 0, top[part_rows], total[part_rows]))
            row_top, row_total = stats[0:1], stats[1:2]
            quarters = out_ref.shape[0] // 2
            first = (2 * k + h + quarters // 2) % quarters
            for p in range(2):
                if p:
                    row_top, row_total = (jnp.concatenate([v[:, half:], v[:, :half]], axis=1) for v in (row_top, row_total))
                start = h * size + p * half
                out_ref[p * quarters + first, 0:half, :] = attended[start : start + half]
                out_ref[p * quarters + first, half:, :] = pack_stats(row_top, row_total)

    tops = []
    for k in range(heads):
        q = jnp.concatenate([ordered(k, 0), ordered(k, 1)], axis=0)
        fresh = jnp.where(allow, dot_nt(q, fresh_keys[k]), NEG)
        part = jnp.full((rows, 128), NEG, F32)
        for c in range(slots // chunk):
            s = dot_nt(q, keys[k, pl.ds(c * chunk, chunk), :])
            s = jnp.where(iota((1, chunk), 1) + c * chunk < valid, s, NEG)
            scores[k, :, pl.ds(c * chunk, chunk)] = s
            for i in range(chunk // 128):
                part = jnp.maximum(part, s[:, i * 128 : (i + 1) * 128])
        top = jnp.maximum(jnp.max(part, axis=1, keepdims=True), jnp.max(fresh, axis=1, keepdims=True))
        tops.append((top, fresh))
    for k in range(heads):
        top, fresh = tops[k]
        weights = jnp.exp2((fresh - top) * rate).astype(BF)
        fresh_ones = jnp.concatenate([fresh_values[k], jnp.ones((NEW, size), BF)], axis=1)
        acc = jnp.dot(weights, fresh_ones, preferred_element_type=F32)
        for c in range(slots // chunk):
            w = jnp.exp2((scores[k, :, pl.ds(c * chunk, chunk)] - top) * rate).astype(BF)
            v = jnp.concatenate([values[k, pl.ds(c * chunk, chunk), :], jnp.ones((chunk, size), BF)], axis=1)
            acc = acc + jnp.dot(w, v, preferred_element_type=F32)
        finish(k, acc, top)


def combine_kernel(r_ref, out_ref, *, rate, last):
    sources = r_ref.shape[0]
    copies = out_ref.shape[0]
    rows = r_ref.shape[1] - STAT_ROWS
    size = r_ref.shape[2]
    stats = [unpack_stats(r_ref[s, rows:, :]) for s in range(sources)]
    top = functools.reduce(jnp.maximum, [m for m, _ in stats])
    weights = [t * jnp.exp2((m - top) * rate) for m, t in stats]
    total = functools.reduce(jnp.add, weights)
    at = iota((size, size), 0)
    factors = jnp.zeros((size, size), F32)
    for s in range(sources):
        factors = jnp.where(at == s, weights[s] / total, factors)
    factors = jnp.transpose(factors)
    out = jnp.zeros((rows, size), F32)
    for s in range(sources):
        out = out + factors[0:rows, s : s + 1] * r_ref[s, 0:rows, :].astype(F32)
    out = out.astype(BF)
    tail = None if last else pack_stats(top, total)
    for c in range(copies):
        out_ref[c, 0:rows, :] = out
        if not last:
            out_ref[c, rows:, :] = tail


def project_kernel(r_ref, w_ref, out_ref):
    n_z, n_x, n_y, rows, size = r_ref.shape
    per = rows // NEW
    acc = jnp.zeros((n_y * NEW, w_ref.shape[1]), F32)
    for x in range(n_x):
        for z in range(n_z):
            for j in range(0, per, 2):
                block = jnp.concatenate(
                    [
                        jnp.concatenate([r_ref[z, (x + n_x // 2) % n_x, (y + n_y // 2) % n_y, pl.ds((j + i) * NEW, NEW), :] for y in range(n_y)], axis=0)
                        for i in range(2)
                    ],
                    axis=1,
                )
                start = ((x * n_z + z) * per + j) * size
                acc = acc + jnp.dot(block, w_ref[pl.ds(start, 2 * size), :], preferred_element_type=F32)
    out_ref[...] = acc.astype(BF).reshape(out_ref.shape)


def listed(count, flip):
    return [[n ^ flip for n in range(count)]]


def in_vmem(n):
    return [pl.BlockSpec(memory_space=pltpu.VMEM)] * n


def stage_kernel(*refs):
    count = (len(refs) - 1) // 2
    copies = [pltpu.make_async_copy(refs[n], refs[count + n], refs[-1].at[n]) for n in range(count)]
    for copy in copies:
        copy.start()
    for copy in copies:
        copy.wait()


def stage(*arrays):
    return pl.pallas_call(
        stage_kernel,
        out_shape=[jax.ShapeDtypeStruct(a.shape, a.dtype) for a in arrays],
        in_specs=[pl.BlockSpec(memory_space=pltpu.HBM)] * len(arrays),
        out_specs=in_vmem(len(arrays)),
        scratch_shapes=[pltpu.SemaphoreType.DMA((len(arrays),))],
        compiler_params=pltpu.CompilerParams(vmem_limit_bytes=8 << 20),
        cost_estimate=pl.CostEstimate(flops=0, bytes_accessed=2 * sum(a.size * 2 for a in arrays), transcendentals=0),
        name="stage",
    )(*[pltpu.with_memory_space_constraint(a, pltpu.HBM) for a in arrays])


def attend(length, q, keys, values, fresh_keys, fresh_values, pos):
    heads, slots, size = keys.shape
    rate = math.log2(math.e) / size**0.5
    chunk = min(slots, 256)
    flops = 4 * heads * NEW * QPK * slots * size
    return pl.pallas_call(
        functools.partial(attend_kernel, rate=rate, chunk=chunk),
        out_shape=jax.ShapeDtypeStruct((4 * heads, size // 2 + STAT_ROWS, size), BF),
        in_specs=[pl.BlockSpec(memory_space=pltpu.SMEM)] + in_vmem(6),
        out_specs=pl.BlockSpec(memory_space=pltpu.VMEM),
        scratch_shapes=[pltpu.VMEM((heads, NEW * QPK, slots), F32)],
        compiler_params=pltpu.CompilerParams(vmem_limit_bytes=13 << 20),
        cost_estimate=pl.CostEstimate(
            flops=flops, bytes_accessed=2 * heads * slots * size * 2, transcendentals=heads * NEW * QPK * slots
        ),
        name="attend",
    )(length, q, keys, values, fresh_keys, fresh_values, pos)


def combine(r, copies, last, rate):
    rows = r.shape[1] - STAT_ROWS if last else r.shape[1]
    return pl.pallas_call(
        functools.partial(combine_kernel, rate=rate, last=last),
        out_shape=jax.ShapeDtypeStruct((copies, rows, r.shape[2]), BF),
        in_specs=in_vmem(1),
        out_specs=pl.BlockSpec(memory_space=pltpu.VMEM),
        compiler_params=pltpu.CompilerParams(vmem_limit_bytes=8 << 20),
        name="combine_last" if last else "combine",
    )(r)


def project(r, w):
    return pl.pallas_call(
        project_kernel,
        out_shape=jax.ShapeDtypeStruct((r.shape[1], NEW, w.shape[1]), BF),
        in_specs=in_vmem(2),
        out_specs=pl.BlockSpec(memory_space=pltpu.VMEM),
        compiler_params=pltpu.CompilerParams(vmem_limit_bytes=8 << 20),
        name="project",
    )(r, w)


def total_kernel(every, out_ref):
    mine = lax.axis_index(HEAD)
    total = every[0, mine].astype(F32)
    for h in range(1, every.shape[0]):
        total = total + every[h, mine].astype(F32)
    out_ref[0] = total.astype(BF)


def total_of(every):
    return pl.pallas_call(
        total_kernel,
        out_shape=jax.ShapeDtypeStruct((1,) + every.shape[2:], BF),
        in_specs=in_vmem(1),
        out_specs=pl.BlockSpec(memory_space=pltpu.VMEM),
        compiler_params=pltpu.CompilerParams(vmem_limit_bytes=2 << 20),
        name="total",
    )(every)


def body(queries, cache_keys, cache_values, new_keys, new_values, lengths, positions, out_weight):
    size = cache_keys.shape[3]
    rate = math.log2(math.e) / size**0.5
    n_ctx = lax.axis_size(CTX)
    mine = queries[0].reshape(1, -1, size)
    sent = jnp.broadcast_to(mine, (n_ctx,) + mine.shape[1:])
    q = lax.all_to_all(sent, Z + ("x",), 0, 0, axis_index_groups=listed(n_ctx, 22), tiled=True)
    staged = stage(cache_keys[0], cache_values[0], new_keys[0], new_values[0], positions)
    part = attend(lengths, q, *staged)
    part = lax.all_to_all(part, ("zb", "x"), 0, 0, axis_index_groups=listed(part.shape[0], 2), tiled=True)
    part = combine(part, lax.axis_size("za"), False, rate)
    last_first = [[(n - 1) % part.shape[0] for n in range(part.shape[0])]]
    part = lax.all_to_all(part, "za", 0, 0, axis_index_groups=last_first, tiled=True)
    spread = ("zb", "x", "y")
    sizes = tuple(lax.axis_size(a) for a in spread)
    rows = combine(part, math.prod(sizes), True, rate)
    rows = lax.all_to_all(rows, spread, 0, 0, axis_index_groups=listed(rows.shape[0], 10), tiled=True)
    out = project(rows.reshape(*sizes, *rows.shape[1:]), out_weight)
    every = lax.all_gather(out, HEAD, axis=0, axis_index_groups=listed(lax.axis_size(HEAD), 2))
    return total_of(every)


def solution(mesh):
    fine = Mesh(mesh.devices.reshape(4, 4, 2, 2, 2, 4), ("x", "za", "zb", "zh", "core", "y"))
    in_specs = (
        P("y", HEAD, CTX, None),
        P("y", HEAD, CTX, None),
        P("y", HEAD, CTX, None),
        P("y", HEAD, None, None),
        P("y", HEAD, None, None),
        P("y"),
        P("y", None),
        P(HEAD, CTX + ("y",)),
    )
    out_specs = P(HEAD, None, CTX + ("y",))
    return jax.shard_map(body, mesh=fine, in_specs=in_specs, out_specs=out_specs, check_vma=False)
```
